32 devices in a mesh: dp: 2 (over x), seq: 16 (over z, y, core).
Axes of the slice: x: 2, y: 2, z: 4, core: 2. Of those that a mesh axis runs over, the one named last changes fastest.
Arguments:
- tokens: bfloat16 [2, 2048, 1024], P('dp', 'seq'), may hold values from -6 to 6
- in_gain: float32 [1024], replicated, may hold values from 0.1 to 1.9
- w_proj: bfloat16 [1024, 4096], replicated, may hold values from -0.1875 to 0.1875
- out_gain: float32 [1024], replicated, may hold values from 0.1 to 1.9
- w_out: bfloat16 [1024, 1024], replicated, may hold values from -0.1875 to 0.1875
- rab_slope: float32 [8], replicated, may hold values from -1 to 0.2
- hist_blocks: int32 [2, 3], P('dp'), may hold values from 1 to 10, 16 in all within a row
- hist_tail: int32 [2, 3], P('dp'), may hold values from 1 to 128
- node_table: bfloat16 [512, 1024], P('dp'), may hold values from -0.1875 to 0.1875
- subtree_map: int32 [8], replicated, may hold values from 0 to 7, each once
- beam_nodes: int32 [6, 1024], P('dp', 'seq'), may hold values from 0 to 511
Outputs:
- layer_out: bfloat16 [2, 2048, 1024], P('dp', 'seq')
- beam_scores: float32 [6, 1024], P('dp', 'seq')
The draws below stay inside these ranges and needn't reach their ends.
Inputs may be any that keep to these rules, and one draw needn't show every extreme that they name: `hist_blocks`: each row sums to 16; its largest entry is exactly 10. `subtree_map`: a permutation of 0 to 7.
All inputs are finite; a program needn't handle non-finite values.
Results may differ from the reference program's by a relative error of at most 0.0059.
Values may be sent and summed in bfloat16 or wider, within the bound.
A program may use at most 128 MiB of HBM per device.

```python
import math
import jax
import jax.numpy as jnp
import numpy as np
from jax import lax

D = 1024
HEADS = 8
HD = 128
BLK = 128
SUBT = 64
USERS = 3
BEAM = 1024
TOK_DP = 2048
NBLK = 16
MOST = 10
USERS_ALL = 6
NODES = 512
SUBTREES = 8
N_DP = 2


def draw_w_proj(key, part):
    entries = jax.random.truncated_normal(key, -6.0, 6.0, (D, 4 * D), jnp.float32)
    return (entries * D ** (-0.5)).astype(jnp.bfloat16)


def draw_rab_slope(key, part):
    return jax.random.uniform(key, (HEADS,), jnp.float32, -0.4, 0.2)


def place_ends(array, stream_key, least, top_value):
    shape = array.shape
    spot = [jax.random.randint(jax.random.fold_in(stream_key, axis), (), 0, shape[axis]) for axis in range(len(shape))]
    array = array.at[tuple(spot)].set(least)
    longest = shape.index(max(shape))
    spot[longest] = (spot[longest] + 1) % shape[longest]
    return array.at[tuple(spot)].set(top_value)


def block_scale(stream_key, shape, shards, least, top_value):
    level = 1.0
    for axis_at, parts in shards:
        steps = jax.random.uniform(jax.random.fold_in(jax.random.fold_in(stream_key, 6), axis_at), (parts,), jnp.float32, least / len(shards), top_value / len(shards))
        level = level * jnp.repeat(jnp.exp(steps), shape[axis_at] // parts).reshape((-1,) + (1,) * (len(shape) - 1 - axis_at))
    return level


def cumulative_ranks(amount, slope):
    portions = [(1 << 20) // math.isqrt(standing ** slope) + 1 for standing in range(1, amount + 1)]
    scale = 1 + sum(portions) // (1 << 30)
    return np.cumsum(np.array([max(1, weight // scale) for weight in portions]))


def ranked(key, dims, count, skew):
    listing = cumulative_ranks(count, skew)
    ticket = jax.random.randint(jax.random.fold_in(key, 1), dims, 0, int(listing[count - 1]))
    grade = jnp.searchsorted(jnp.asarray(listing, jnp.int32), ticket, side="right")
    return jax.random.permutation(jax.random.fold_in(key, 2), count)[grade].astype(jnp.int32)


def split_up(count, total, limit, skew):
    loads = [(1 << 20) // math.isqrt(standing ** skew) + 1 for standing in range(2, count + 1)]
    surplus, holding = total - limit - (count - 1), [1] * (count - 1)
    while surplus > 0:
        movable = [i for i in range(count - 1) if holding[i] < limit]
        pool, remaining = sum([loads[i] for i in movable]), surplus
        for i in movable:
            more = min(limit - holding[i], max(1, remaining * loads[i] // pool), surplus)
            holding[i] = holding[i] + more
            surplus = surplus - more
    return np.array([limit] + holding)


def uneven(stream_key, amount, total, limit, slope):
    if amount == 2:
        one = jax.random.randint(stream_key, (), max(1, total - limit), min(limit, total - 1) + 1)
        return jnp.stack([one, total - one])
    sizes = jnp.asarray(split_up(amount, total, limit, slope), jnp.int32)
    pairs = (amount - 1) // 2
    source_of, receiver = sizes[1:1 + 2 * pairs:2], sizes[2:2 + 2 * pairs:2]
    slack = jnp.minimum(source_of - 1, limit - receiver)
    shifted = jax.random.randint(jax.random.fold_in(stream_key, 1), (pairs,), 0, 1 << 20) % (slack + 1)
    sizes = sizes.at[1:1 + 2 * pairs:2].set(source_of - shifted).at[2:2 + 2 * pairs:2].set(receiver + shifted)
    return sizes[jax.random.permutation(jax.random.fold_in(stream_key, 2), amount)]


def scatter_about(rng, shape, width, reach, split=(), held_as=jnp.bfloat16):
    level = block_scale(rng, shape, split, -0.22, 0.18) if split else 1.0
    values = jax.random.normal(rng, shape, jnp.float32) * width * level
    return jnp.minimum(jnp.maximum(values, -reach), reach).astype(held_as)


def setup_inputs(seed: int = 0) -> dict:
    key_list = jax.random.split(jax.random.key(seed), 12)
    tokens = scatter_about(key_list[0], (N_DP, TOK_DP, D), 1.0, 6.0, ((0, 2), (1, 16)))
    in_gain = jnp.clip(1.0 + 0.18 * jax.random.normal(key_list[1], (D,), jnp.float32), 0.1, 1.9)
    w_proj = draw_w_proj(jax.random.fold_in(key_list[11], 71), 0)
    out_gain = jnp.clip(1.0 + 0.18 * jax.random.normal(key_list[3], (D,), jnp.float32), 0.1, 1.9)
    w_out = scatter_about(key_list[4], (D, D), D ** -0.5, 0.1875)
    rab_slope = draw_rab_slope(jax.random.fold_in(key_list[11], 71), 0)
    hist_blocks = jax.vmap(lambda own: uneven(own, USERS, NBLK, MOST, 0))(jax.random.split(key_list[6], N_DP)).reshape((N_DP, USERS)).astype(jnp.int32)
    hist_tail = place_ends(jax.random.randint(key_list[7], (N_DP, USERS), 1, BLK + 1), jax.random.fold_in(key_list[7], 1), 1, BLK).astype(jnp.int32)
    node_table = scatter_about(key_list[8], (NODES, D), D ** -0.5, 0.1875, ((0, 2),))
    subtree_map = jax.random.permutation(key_list[9], SUBTREES).astype(jnp.int32)
    beam_nodes = place_ends(ranked(key_list[10], (USERS_ALL, BEAM), NODES, 1), jax.random.fold_in(key_list[10], 3), 0, NODES - 1).astype(jnp.int32)
    return {"tokens": tokens, "in_gain": in_gain, "w_proj": w_proj, "out_gain": out_gain, "w_out": w_out, "rab_slope": rab_slope, "hist_blocks": hist_blocks, "hist_tail": hist_tail, "node_table": node_table, "subtree_map": subtree_map, "beam_nodes": beam_nodes}


def layer_norm(rows):
    centred = rows - lax.optimization_barrier(jnp.mean(rows, axis=-1, keepdims=True))
    spread = lax.optimization_barrier(jnp.mean(centred * centred, axis=-1, keepdims=True))
    return centred * lax.rsqrt(spread + 1e-05)

def user_table(blocks, tail_len):
    blocks = blocks.astype(jnp.int32)
    starts = (jnp.cumsum(blocks) - blocks).astype(jnp.int32)
    lengths = ((blocks - 1) * BLK + tail_len.astype(jnp.int32)).astype(jnp.int32)
    return (starts, lengths)

def segments(blocks, tail_len, positions):
    starts, lengths = user_table(blocks, tail_len)
    block_of = jnp.floor_divide(positions, BLK).astype(jnp.int32)
    owning = lax.optimization_barrier(jnp.sum((block_of[:, None] >= starts[None, :]).astype(jnp.int32), axis=1)) - 1
    onehot = (owning[:, None] == jnp.arange(USERS, dtype=jnp.int32)[None, :]).astype(jnp.int32)
    first_pos = lax.optimization_barrier(jnp.sum(onehot * starts[None, :], axis=1)) * BLK
    user_len = lax.optimization_barrier(jnp.sum(onehot * lengths[None, :], axis=1))
    is_live = (owning >= 0) & (positions - first_pos < user_len)
    return jnp.where(is_live, owning, -1).astype(jnp.int32)

def attend(query_rows, query_pos, query_seg, key_rows, value_rows, key_pos, key_seg, rab_slope):
    scores = jnp.einsum('qhd,khd->hqk', query_rows.astype(jnp.float32), key_rows.astype(jnp.float32))
    scores = scores * query_rows.shape[-1] ** (-0.5)
    gap = query_pos[:, None] - key_pos[None, :]
    allowed = (query_seg[:, None] == key_seg[None, :]) & (query_seg[:, None] >= 0) & (gap >= 0)
    bias = rab_slope[:, None, None] * jnp.log1p(jnp.maximum(gap, 0).astype(jnp.float32))[None]
    weights = jnp.where(allowed[None], jax.nn.silu(scores + bias), 0.0).astype(jnp.bfloat16)
    return jnp.einsum('hqk,khd->qhd', weights.astype(jnp.float32), value_rows.astype(jnp.float32))

def reference(tokens, in_gain, w_proj, out_gain, w_out, rab_slope, hist_blocks, hist_tail, node_table, subtree_map, beam_nodes):
    back = MOST * BLK
    qblock = math.gcd(512, TOK_DP)

    def one_group(item):
        x_rows, blocks, tail_len = item
        normed = (layer_norm(x_rows.astype(jnp.float32)) * in_gain).astype(jnp.bfloat16)
        proj = jax.nn.silu(jnp.dot(normed, w_proj, preferred_element_type=jnp.float32)).astype(jnp.bfloat16)
        gate_rows = proj[:, :D]
        query_rows = proj[:, D:2 * D]
        key_rows = proj[:, 2 * D:3 * D]
        value_rows = proj[:, 3 * D:]
        positions = jnp.arange(TOK_DP, dtype=jnp.int32)
        seg_all = segments(blocks, tail_len, positions)
        key_pad = jnp.concatenate([jnp.zeros((back, D), jnp.bfloat16), key_rows], axis=0)
        value_pad = jnp.concatenate([jnp.zeros((back, D), jnp.bfloat16), value_rows], axis=0)
        pos_pad = jnp.arange(-back, TOK_DP, dtype=jnp.int32)
        seg_pad = jnp.concatenate([jnp.full((back,), -1, jnp.int32), seg_all], axis=0)

        def per_block(index):
            start = (index * qblock).astype(jnp.int32)
            span = back + qblock
            queries = lax.dynamic_slice_in_dim(query_rows, start, qblock, 0).reshape(qblock, HEADS, HD)
            query_pos = lax.dynamic_slice_in_dim(positions, start, qblock, 0)
            query_seg = lax.dynamic_slice_in_dim(seg_all, start, qblock, 0)
            keys_here = lax.dynamic_slice_in_dim(key_pad, start, span, 0).reshape(span, HEADS, HD)
            values_here = lax.dynamic_slice_in_dim(value_pad, start, span, 0).reshape(span, HEADS, HD)
            key_pos = lax.dynamic_slice_in_dim(pos_pad, start, span, 0)
            key_seg = lax.dynamic_slice_in_dim(seg_pad, start, span, 0)
            return attend(queries, query_pos, query_seg, keys_here, values_here, key_pos, key_seg, rab_slope)
        mixed = lax.map(per_block, jnp.arange(TOK_DP // qblock, dtype=jnp.int32)).reshape(TOK_DP, D)
        gated = (layer_norm(mixed) * out_gain * gate_rows.astype(jnp.float32)).astype(jnp.bfloat16)
        layer_rows = (x_rows.astype(jnp.float32) + jnp.dot(gated, w_out, preferred_element_type=jnp.float32)).astype(jnp.bfloat16)
        starts, lengths = user_table(blocks, tail_len)
        last_slot = (starts * BLK + lengths - 1).astype(jnp.int32)
        states = jnp.take(layer_rows, last_slot, axis=0)
        return (layer_rows, states)
    layer_out, states = lax.map(one_group, (tokens, hist_blocks, hist_tail))
    all_states = states.reshape(USERS_ALL, D)
    stored = (jnp.take(subtree_map, beam_nodes // SUBT) * SUBT + beam_nodes % SUBT).astype(jnp.int32)

    def score_user(item):
        state_row, row_ids = item
        return jnp.dot(jnp.take(node_table, row_ids, axis=0), state_row, preferred_element_type=jnp.float32)
    beam_scores = lax.map(score_user, (all_states, stored))
    return (layer_out, beam_scores)
```

```python
import functools

import jax
import jax.numpy as jnp
from jax import lax
from jax.experimental import pallas as pl
from jax.experimental.pallas import tpu as pltpu
from jax.sharding import PartitionSpec as P

BLK = 128
SUBT = 64
USERS = 3
LANES = 128
MESH = pl.DeviceIdType.MESH
OFF = -1e30


def layer_norm(rows):
    centred = rows - jnp.mean(rows, axis=-1, keepdims=True)
    spread = jnp.mean(centred * centred, axis=-1, keepdims=True)
    return centred * lax.rsqrt(spread + 1e-05)


def silu_of_half(half):
    return half + half * jnp.tanh(half)


def far_first(count):
    order = []
    for step in range(count // 2):
        for offset in (count // 2 - step, count // 2 + step):
            if 0 < offset < count and offset not in order:
                order.append(offset)
    return order


def layer_kernel(
    n_dp,
    n_seq,
    x_ref,
    in_gain_ref,
    w_proj_ref,
    out_gain_ref,
    w_out_ref,
    slope_ref,
    blocks_ref,
    tail_ref,
    table_ref,
    map_ref,
    beam_ref,
    layer_ref,
    scores_ref,
    w_buf,
    w_out_buf,
    table_buf,
    sent,
    gate,
    kv,
    query,
    result,
    mix,
    bias,
    part_sent,
    part_recv,
    onehot,
    w_sem,
    w_out_sem,
    table_sem,
    table_send,
    table_recv,
    kv_send,
    kv_recv,
    fwd_send,
    q_send,
    q_recv,
    r_send,
    r_recv,
    p_send,
    p_recv,
):
    tok, width = x_ref.shape[1:]
    heads, _, head_dim = mix.shape
    half = query.shape[1]
    window = bias.shape[1] // tok
    nodes = table_ref.shape[0]
    chunks = n_dp * nodes // LANES
    me = lax.axis_index("seq")
    dp = lax.axis_index("dp")
    chip, core = me // 2, me % 2
    sibling = chip * 2 + (1 - core)

    def remote(src, dst, send_sem, recv_sem, where):
        return pltpu.make_async_remote_copy(
            src_ref=src,
            dst_ref=dst,
            send_sem=send_sem,
            recv_sem=recv_sem,
            device_id=where,
            device_id_type=MESH,
        )

    order = (2, 3, 1, 0)
    w_copies = {
        part: pltpu.make_async_copy(
            w_proj_ref.at[:, pl.ds(part * width, width)], w_buf.at[part], w_sem.at[part]
        )
        for part in order
    }
    for part in order:
        w_copies[part].start()

    barrier = pltpu.get_barrier_semaphore()
    for step in range(1, n_seq):
        pl.semaphore_signal(
            barrier, inc=1, device_id={"seq": (me + step) % n_seq}, device_id_type=MESH
        )
    for step in range(1, n_dp):
        pl.semaphore_signal(
            barrier, inc=1, device_id={"dp": (dp + step) % n_dp}, device_id_type=MESH
        )

    x_rows = x_ref[0].astype(jnp.float32)
    normed = (layer_norm(x_rows) * in_gain_ref[...]).astype(jnp.bfloat16)

    def project(part, store):
        w_copies[part].wait()
        for piece in range(heads // 2):
            columns = pl.ds(piece * 2 * head_dim, 2 * head_dim)
            out = jnp.dot(normed, w_buf[part, :, columns], preferred_element_type=jnp.float32)
            store(piece, silu_of_half(0.5 * out).astype(jnp.bfloat16))

    def store_heads(slot):
        def store(piece, rows):
            sent[slot, 2 * piece] = rows[:, :head_dim]
            sent[slot, 2 * piece + 1] = rows[:, head_dim:]

        return store

    chip_order = far_first(heads)
    waits = []
    for which in range(2):
        slot = which + 1
        project(slot + 1, store_heads(slot))
        if which == 0:
            pl.semaphore_wait(barrier, n_seq - 1 + n_dp - 1)
        for step in chip_order:
            head = (chip + step) % heads
            copy = remote(
                sent.at[slot, head],
                kv.at[which, me],
                kv_send.at[which, step],
                kv_recv.at[which, me],
                {"seq": head * 2 + core},
            )
            copy.start()
            waits.append(copy)
        copy = remote(
            sent.at[slot, chip],
            kv.at[which, me],
            kv_send.at[which, 0],
            kv_recv.at[which, me],
            {"seq": sibling},
        )
        copy.start()
        waits.append(copy)
        pltpu.make_async_copy(
            sent.at[slot, chip], kv.at[which, me], kv_recv.at[which, me]
        ).start()

    project(1, store_heads(0))
    for step in chip_order:
        head = (chip + step) % heads
        for part in range(2):
            copy = remote(
                sent.at[0, head, pl.ds(part * half, half)],
                query.at[me],
                q_send.at[2 * step + part],
                q_recv.at[me],
                {"seq": head * 2 + part},
            )
            copy.start()
            waits.append(copy)
    copy = remote(
        sent.at[0, chip, pl.ds((1 - core) * half, half)],
        query.at[me],
        q_send.at[0],
        q_recv.at[me],
        {"seq": sibling},
    )
    copy.start()
    waits.append(copy)
    pltpu.make_async_copy(
        sent.at[0, chip, pl.ds(core * half, half)], query.at[me], q_recv.at[me]
    ).start()

    for step in range(1, n_dp):
        copy = remote(
            table_ref,
            table_buf.at[dp],
            table_send.at[step],
            table_recv.at[dp],
            {"dp": (dp + step) % n_dp},
        )
        copy.start()
        waits.append(copy)
    pltpu.make_async_copy(table_ref, table_buf.at[dp], table_sem).start()
    w_out_copy = pltpu.make_async_copy(w_out_ref, w_out_buf, w_out_sem)
    w_out_copy.start()

    def store_gate(piece, rows):
        gate[:, pl.ds(piece * 2 * head_dim, 2 * head_dim)] = rows

    project(0, store_gate)

    row = lax.broadcasted_iota(jnp.int32, bias.shape, 0)
    column = lax.broadcasted_iota(jnp.int32, bias.shape, 1)
    gap = (window - 1) * tok + core * half + row - column
    slope = slope_ref[chip]
    logs = jnp.log(1.0 + jnp.maximum(gap, 0).astype(jnp.float32))
    bias[...] = jnp.where(gap >= 0, (0.5 * slope) * logs, OFF)

    beams = beam_ref[...]
    subtree = beams >> 6
    base = jnp.zeros_like(beams)
    for index in range(map_ref.shape[0]):
        base = jnp.where(subtree == index, map_ref[index], base)
    stored = base * SUBT + (beams & (SUBT - 1))
    per_user = beams.shape[1]
    stored_row = jnp.concatenate([stored[u : u + 1] for u in range(USERS)], axis=1)
    node = lax.broadcasted_iota(jnp.int32, onehot.shape, 0)
    onehot[...] = jnp.where(node == stored_row, 1.0, 0.0).astype(jnp.bfloat16)

    starts = [0, blocks_ref[0, 0], blocks_ref[0, 0] + blocks_ref[0, 1]]
    lengths = [(blocks_ref[0, u] - 1) * BLK + tail_ref[0, u] for u in range(USERS)]

    def attend(block):
        pltpu.make_async_copy(query.at[block], query.at[block], q_recv.at[block]).wait()
        count = min(block + 1, window)
        low = block + 1 - count
        keys = kv[0, low : block + 1].reshape(count * tok, head_dim)
        values = kv[1, low : block + 1].reshape(count * tok, head_dim)
        first = jnp.where(block >= starts[1], starts[1], 0)
        length = jnp.where(block >= starts[1], lengths[1], lengths[0])
        first = jnp.where(block >= starts[2], starts[2], first)
        length = jnp.where(block >= starts[2], lengths[2], length)
        column = lax.broadcasted_iota(jnp.int32, (1, count * tok), 1) + low * tok
        seen = jnp.where(column >= first * tok, 0.0, OFF)
        scores = lax.dot_general(
            query[block], keys, (((1,), (1,)), ((), ())), preferred_element_type=jnp.float32
        )
        halves = scores * (0.5 * head_dim ** (-0.5)) + bias[:, (window - count) * tok :] + seen
        weights = silu_of_half(halves).astype(jnp.bfloat16)
        out = jnp.dot(weights, values, preferred_element_type=jnp.float32)
        row = lax.broadcasted_iota(jnp.int32, (half, head_dim), 0)
        live = (block - first) * tok + core * half + row < length
        result[block] = jnp.where(live, out, 0.0).astype(jnp.bfloat16)
        landing = mix.at[chip, pl.ds(core * half, half)]

        @pl.when(me != block)
        def _():
            remote(
                result.at[block], landing, r_send.at[block], r_recv.at[me], {"seq": block}
            ).start()

        @pl.when(me == block)
        def _():
            pltpu.make_async_copy(result.at[block], landing, r_recv.at[me]).start()

    def attend_chip(other):
        for which in range(2):
            relayed = 2 * other + (1 - core)
            pltpu.make_async_copy(
                kv.at[which, relayed], kv.at[which, relayed], kv_recv.at[which, relayed]
            ).wait()
        for block in (2 * other, 2 * other + 1):
            attend(block)

    for other in range(heads):
        direct = 2 * other + core
        for which in range(2):
            landed = kv.at[which, direct]
            pltpu.make_async_copy(landed, landed, kv_recv.at[which, direct]).wait()

            @pl.when(other != chip)
            def _():
                remote(
                    landed,
                    landed,
                    fwd_send.at[which, other],
                    kv_recv.at[which, direct],
                    {"seq": sibling},
                ).start()

        if other > 0:
            attend_chip(other - 1)
    attend_chip(heads - 1)

    w_out_copy.wait()
    for source in range(n_seq):
        landing = mix.at[source // 2, pl.ds((source % 2) * half, half)]
        pltpu.make_async_copy(landing, landing, r_recv.at[source]).wait()
    mixed = jnp.concatenate([mix[head] for head in range(heads)], axis=1).astype(jnp.float32)
    gated = layer_norm(mixed) * out_gain_ref[...] * gate[...].astype(jnp.float32)
    out = jnp.dot(
        gated.astype(jnp.bfloat16), w_out_buf[...], preferred_element_type=jnp.float32
    )
    layer_rows = (x_ref[0].astype(jnp.float32) + out).astype(jnp.bfloat16)
    layer_ref[0] = layer_rows

    rows = 16
    which_user = lax.broadcasted_iota(jnp.int32, (rows, tok), 0)
    slot = lax.broadcasted_iota(jnp.int32, (rows, tok), 1) + me * tok
    last = jnp.full((rows, tok), -1, jnp.int32)
    for u in range(USERS):
        last = jnp.where(which_user == u, starts[u] * BLK + lengths[u] - 1, last)
    picker = jnp.where(slot == last, 1.0, 0.0).astype(jnp.bfloat16)
    states = jnp.dot(picker, layer_rows, preferred_element_type=jnp.float32).astype(jnp.bfloat16)
    pltpu.make_async_copy(table_ref, table_buf.at[dp], table_sem).wait()
    for step in range(1, n_dp):
        source = (dp + step) % n_dp
        pltpu.make_async_copy(
            table_buf.at[source], table_buf.at[source], table_recv.at[source]
        ).wait()
    node_scores = lax.dot_general(
        states,
        table_buf[...].reshape(n_dp * nodes, width),
        (((1,), (1,)), ((), ())),
        preferred_element_type=jnp.float32,
    )
    pieces = [
        node_scores[u : u + 1, c * LANES : (c + 1) * LANES]
        for u in range(USERS)
        for c in range(chunks)
    ]
    spare = part_sent.shape[0] - len(pieces)
    if spare:
        pieces.append(jnp.zeros((spare, LANES), jnp.float32))
    part = jnp.concatenate(pieces, axis=0).astype(jnp.bfloat16)
    part_sent[...] = part
    part_recv[me] = part
    for step in far_first(n_seq):
        copy = remote(
            part_sent,
            part_recv.at[me],
            p_send.at[step],
            p_recv.at[me],
            {"seq": (me + step) % n_seq},
        )
        copy.start()
        waits.append(copy)

    for copy in waits:
        copy.wait_send()
    for other in range(heads):
        direct = 2 * other + core

        @pl.when(other != chip)
        def _():
            for which in range(2):
                remote(
                    kv.at[which, direct],
                    kv.at[which, direct],
                    fwd_send.at[which, other],
                    kv_recv.at[which, direct],
                    {"seq": sibling},
                ).wait_send()

    for block in range(n_seq):

        @pl.when(me != block)
        def _():
            remote(
                result.at[block],
                mix.at[chip, pl.ds(core * half, half)],
                r_send.at[block],
                r_recv.at[me],
                {"seq": block},
            ).wait_send()

    for step in far_first(n_seq):
        source = (me + step) % n_seq
        pltpu.make_async_copy(
            part_recv.at[source], part_recv.at[source], p_recv.at[source]
        ).wait()
    total = jnp.sum(part_recv[...].astype(jnp.float32), axis=0)
    users = [
        jnp.concatenate(
            [total[u * chunks + c : u * chunks + c + 1] for c in range(chunks)], axis=1
        )
        for u in range(USERS)
    ]
    users.append(jnp.zeros((rows - USERS, n_dp * nodes), jnp.float32))
    score_rows = jnp.concatenate(users, axis=0).astype(jnp.bfloat16)
    picked = jnp.dot(score_rows, onehot[...], preferred_element_type=jnp.float32)
    for u in range(USERS):
        scores_ref[u : u + 1] = picked[u : u + 1, u * per_user : (u + 1) * per_user]


def body(
    n_dp,
    n_seq,
    tokens,
    in_gain,
    w_proj,
    out_gain,
    w_out,
    rab_slope,
    hist_blocks,
    hist_tail,
    node_table,
    subtree_map,
    beam_nodes,
):
    _, tok, width = tokens.shape
    heads = rab_slope.shape[0]
    head_dim = width // heads
    nodes = node_table.shape[0]
    half = tok // 2
    assert n_seq == 2 * heads and tok == BLK
    window = n_seq // 2 + 2
    part_rows = -(-USERS * n_dp * nodes // LANES // 16) * 16
    vmem = pl.BlockSpec(memory_space=pltpu.VMEM)
    smem = pl.BlockSpec(memory_space=pltpu.SMEM)
    hbm = pl.BlockSpec(memory_space=pl.ANY)
    dma = pltpu.SemaphoreType.DMA
    bf16 = jnp.bfloat16
    return pl.pallas_call(
        functools.partial(layer_kernel, n_dp, n_seq),
        out_shape=(
            jax.ShapeDtypeStruct(tokens.shape, bf16),
            jax.ShapeDtypeStruct(beam_nodes.shape, jnp.float32),
        ),
        in_specs=[vmem, vmem, hbm, vmem, hbm, smem, smem, smem, hbm, smem, vmem],
        out_specs=(vmem, vmem),
        scratch_shapes=[
            pltpu.VMEM((4, width, width), bf16),
            pltpu.VMEM((width, width), bf16),
            pltpu.VMEM((n_dp, nodes, width), bf16),
            pltpu.VMEM((3, heads, tok, head_dim), bf16),
            pltpu.VMEM((tok, width), bf16),
            pltpu.VMEM((2, n_seq, tok, head_dim), bf16),
            pltpu.VMEM((n_seq, half, head_dim), bf16),
            pltpu.VMEM((n_seq, half, head_dim), bf16),
            pltpu.VMEM((heads, tok, head_dim), bf16),
            pltpu.VMEM((half, window * tok), jnp.float32),
            pltpu.VMEM((part_rows, LANES), bf16),
            pltpu.VMEM((n_seq, part_rows, LANES), bf16),
            pltpu.VMEM((n_dp * nodes, USERS * beam_nodes.shape[1]), bf16),
            dma((4,)),
            dma,
            dma,
            dma((n_dp,)),
            dma((n_dp,)),
            dma((2, heads)),
            dma((2, n_seq)),
            dma((2, heads)),
            dma((n_seq,)),
            dma((n_seq,)),
            dma((n_seq,)),
            dma((n_seq,)),
            dma((n_seq,)),
            dma((n_seq,)),
        ],
        compiler_params=pltpu.CompilerParams(
            collective_id=0, has_side_effects=True, vmem_limit_bytes=56 * 1024 * 1024
        ),
    )(
        tokens,
        in_gain.reshape(1, width),
        w_proj,
        out_gain.reshape(1, width),
        w_out,
        rab_slope,
        hist_blocks,
        hist_tail,
        node_table,
        subtree_map,
        beam_nodes,
    )


def solution(mesh):
    placed = (
        P("dp", "seq", None),
        P(),
        P(),
        P(),
        P(),
        P(),
        P("dp", None),
        P("dp", None),
        P("dp", None),
        P(),
        P("dp", "seq"),
    )
    return jax.shard_map(
        functools.partial(body, mesh.shape["dp"], mesh.shape["seq"]),
        mesh=mesh,
        in_specs=placed,
        out_specs=(P("dp", "seq", None), P("dp", "seq")),
        check_vma=False,
    )
```

```python
import functools

import jax
import jax.numpy as jnp
from jax import lax
from jax.experimental import pallas as pl
from jax.experimental.pallas import tpu as pltpu
from jax.sharding import PartitionSpec as P

BLK = 128
SUBT = 64
USERS = 3
LANES = 128
MESH = pl.DeviceIdType.MESH
OFF = -1e30


def layer_norm(rows):
    centred = rows - jnp.mean(rows, axis=-1, keepdims=True)
    spread = jnp.mean(centred * centred, axis=-1, keepdims=True)
    return centred * lax.rsqrt(spread + 1e-05)


def silu_of_half(half):
    return half + half * jnp.tanh(half)


def far_first(count):
    order = []
    for step in range(count // 2):
        for offset in (count // 2 - step, count // 2 + step):
            if 0 < offset < count and offset not in order:
                order.append(offset)
    return order


def layer_kernel(
    n_dp,
    n_seq,
    x_hbm,
    in_gain_ref,
    w_proj_ref,
    out_gain_ref,
    w_out_ref,
    slope_ref,
    blocks_ref,
    tail_ref,
    table_ref,
    map_ref,
    beam_ref,
    layer_ref,
    scores_ref,
    x_ref,
    w_buf,
    w_out_buf,
    table_buf,
    sent,
    gate,
    kv,
    query,
    total_ref,
    result,
    mix,
    bias,
    part_sent,
    part_recv,
    onehot,
    x_sem,
    w_sem,
    w_out_sem,
    table_sem,
    table_send,
    table_recv,
    kv_send,
    kv_recv,
    fwd_send,
    q_send,
    q_recv,
    r_send,
    r_recv,
    p_send,
    p_recv,
):
    tok, width = x_ref.shape[1:]
    heads, _, head_dim = mix.shape
    half = query.shape[1]
    nodes = table_ref.shape[0]
    chunks = n_dp * nodes // LANES
    me = lax.axis_index("seq")
    dp = lax.axis_index("dp")
    chip, core = me // 2, me % 2
    sibling = chip * 2 + (1 - core)

    def remote(src, dst, send_sem, recv_sem, where):
        return pltpu.make_async_remote_copy(
            src_ref=src,
            dst_ref=dst,
            send_sem=send_sem,
            recv_sem=recv_sem,
            device_id=where,
            device_id_type=MESH,
        )

    bits = [(chip // (1 << bit)) % 2 for bit in range((heads - 1).bit_length())]

    def partner(step):
        return sum(
            (1 - value if step >> bit & 1 else value) * (1 << bit)
            for bit, value in enumerate(bits)
        )

    x_copy = pltpu.make_async_copy(x_hbm, x_ref, x_sem)
    x_copy.start()
    pieces = heads // 2
    pair = 2 * head_dim
    waves = ((0, pieces - 1), tuple(range(1, pieces - 1)))
    order = [(part, piece) for wave in waves for part in (2, 3, 1) for piece in wave]
    order += [(0, piece) for piece in range(pieces)]
    w_copies = {}
    for part, piece in order:
        copy = pltpu.make_async_copy(
            w_proj_ref.at[:, pl.ds(part * width + piece * pair, pair)],
            w_buf.at[part, piece],
            w_sem.at[part, piece],
        )
        copy.start()
        w_copies[part, piece] = copy

    barrier = pltpu.get_barrier_semaphore()
    for step in range(1, n_seq):
        pl.semaphore_signal(
            barrier, inc=1, device_id={"seq": (me + step) % n_seq}, device_id_type=MESH
        )
    for step in range(1, n_dp):
        pl.semaphore_signal(
            barrier, inc=1, device_id={"dp": (dp + step) % n_dp}, device_id_type=MESH
        )

    x_copy.wait()
    x_rows = x_ref[0].astype(jnp.float32)
    normed = (layer_norm(x_rows) * in_gain_ref[...]).astype(jnp.bfloat16)

    def project(part, piece):
        w_copies[part, piece].wait()
        out = jnp.dot(normed, w_buf[part, piece], preferred_element_type=jnp.float32)
        return silu_of_half(0.5 * out).astype(jnp.bfloat16)

    waits = []
    for wave in waves:
        wave_heads = [2 * piece + odd for piece in wave for odd in range(2)]
        for part in (2, 3, 1):
            slot, which = part - 1, part - 2
            for piece in wave:
                rows = project(part, piece)
                sent[slot, 2 * piece] = rows[:, :head_dim]
                sent[slot, 2 * piece + 1] = rows[:, head_dim:]
            if part == 2 and wave is waves[0]:
                pl.semaphore_wait(barrier, n_seq - 1 + n_dp - 1)
            for head in wave_heads:
                for core_to in range(2):
                    if part == 1:
                        piece_ref = sent.at[0, head, pl.ds(core_to * half, half)]
                        landing, send_sem, recv_sem = query.at[me], q_send, q_recv.at[me]
                        goes = True
                    else:
                        piece_ref, landing = sent.at[slot, head], kv.at[which, me]
                        send_sem, recv_sem = kv_send.at[which], kv_recv.at[which, me]
                        goes = (chip == head) | (core == core_to)
                    here = me == 2 * head + core_to

                    @pl.when(jnp.logical_not(here) & goes)
                    def _():
                        remote(
                            piece_ref,
                            landing,
                            send_sem.at[2 * head + core_to],
                            recv_sem,
                            {"seq": 2 * head + core_to},
                        ).start()

                    @pl.when(here)
                    def _():
                        pltpu.make_async_copy(piece_ref, landing, recv_sem).start()

    for step in range(1, n_dp):
        copy = remote(
            table_ref,
            table_buf.at[dp],
            table_send.at[step],
            table_recv.at[dp],
            {"dp": (dp + step) % n_dp},
        )
        copy.start()
        waits.append(copy)
    pltpu.make_async_copy(table_ref, table_buf.at[dp], table_sem).start()
    w_out_copy = pltpu.make_async_copy(w_out_ref, w_out_buf, w_out_sem)
    w_out_copy.start()

    for piece in range(pieces):
        gate[:, piece * pair : (piece + 1) * pair] = project(0, piece)

    row = lax.broadcasted_iota(jnp.int32, bias.shape, 0)
    column = lax.broadcasted_iota(jnp.int32, bias.shape, 1)
    gap = (row // half) * tok + row % half + core * half - column
    slope = slope_ref[chip]
    logs = jnp.log(1.0 + jnp.maximum(gap, 0).astype(jnp.float32))
    bias[...] = jnp.where(gap >= 0, (0.5 * slope) * logs, OFF)
    total_ref[...] = jnp.zeros_like(total_ref)
    query[n_seq:] = jnp.zeros((query.shape[0] - n_seq, half, head_dim), jnp.bfloat16)

    beams = beam_ref[...]
    subtree = beams >> 6
    base = jnp.zeros_like(beams)
    for index in range(map_ref.shape[0]):
        base = jnp.where(subtree == index, map_ref[index], base)
    stored = base * SUBT + (beams & (SUBT - 1))
    per_user = beams.shape[1]
    stored_row = jnp.concatenate([stored[u : u + 1] for u in range(USERS)], axis=1)
    node = lax.broadcasted_iota(jnp.int32, onehot.shape, 0)
    onehot[...] = jnp.where(node == stored_row, 1.0, 0.0).astype(jnp.bfloat16)

    starts = [0, blocks_ref[0, 0], blocks_ref[0, 0] + blocks_ref[0, 1]]
    lengths = [(blocks_ref[0, u] - 1) * BLK + tail_ref[0, u] for u in range(USERS)]

    def owner(block):
        first = jnp.where(block >= starts[1], starts[1], 0)
        length = jnp.where(block >= starts[1], lengths[1], lengths[0])
        first = jnp.where(block >= starts[2], starts[2], first)
        length = jnp.where(block >= starts[2], lengths[2], length)
        return first, length

    def landed(ref, sem):
        pltpu.make_async_copy(ref, ref, sem).wait()

    span = bias.shape[0] // half
    key_block = lax.broadcasted_iota(jnp.int32, (1, 2 * tok), 1) // tok

    def attend(other):
        block = 2 * other
        queries = query[pl.ds(block, span)].reshape(span * half, head_dim)
        keys = kv[0, pl.ds(block, 2)].reshape(2 * tok, head_dim)
        values = kv[1, pl.ds(block, 2)].reshape(2 * tok, head_dim)
        scores = lax.dot_general(
            queries, keys, (((1,), (1,)), ((), ())), preferred_element_type=jnp.float32
        )
        weights = []
        for ahead in range(span):
            first, _ = owner(block + ahead)
            seen = jnp.where(key_block + block >= first, 0.0, OFF)
            rows = slice(ahead * half, (ahead + 1) * half)
            halves = scores[rows] * (0.5 * head_dim ** (-0.5)) + bias[rows] + seen
            weights.append(silu_of_half(halves).astype(jnp.bfloat16))
        out = jnp.dot(
            jnp.concatenate(weights, axis=0), values, preferred_element_type=jnp.float32
        )
        total_ref[pl.ds(block, span)] += out.reshape(span, half, head_dim)

    def relay(step):
        other = partner(step)
        for which in range(2):
            ref = kv.at[which, 2 * other + core]
            sem = kv_recv.at[which, 2 * other + core]
            landed(ref, sem)
            if step > 0:
                copy = remote(ref, ref, fwd_send.at[which, step], sem, {"seq": sibling})
                copy.start()
                waits.append(copy)

    def attend_relayed(step):
        other = partner(step)
        for which in range(2):
            block = 2 * other + (1 - core)
            landed(kv.at[which, block], kv_recv.at[which, block])
        attend(other)

    relay(0)
    for step in range(1, heads):
        relay(step)
        if step == 1:
            for block in range(n_seq):
                landed(query.at[block], q_recv.at[block])
        attend_relayed(step - 1)
    attend_relayed(heads - 1)

    row = lax.broadcasted_iota(jnp.int32, (half, head_dim), 0)
    landing = mix.at[chip, pl.ds(core * half, half)]
    for step in reversed(range(heads)):
        for part in range(2):
            block = 2 * partner(step) + (core if part == 0 else 1 - core)
            first, length = owner(block)
            live = (block - first) * tok + core * half + row < length
            result[block] = jnp.where(live, total_ref[block], 0.0).astype(jnp.bfloat16)
            if step == 0 and part == 0:
                pltpu.make_async_copy(result.at[block], landing, r_recv.at[me]).start()
            else:
                copy = remote(
                    result.at[block],
                    landing,
                    r_send.at[2 * step + part],
                    r_recv.at[me],
                    {"seq": block},
                )
                copy.start()
                waits.append(copy)

    w_out_copy.wait()
    for source in range(n_seq):
        landing = mix.at[source // 2, pl.ds((source % 2) * half, half)]
        pltpu.make_async_copy(landing, landing, r_recv.at[source]).wait()
    mixed = jnp.concatenate([mix[head] for head in range(heads)], axis=1).astype(jnp.float32)
    gated = layer_norm(mixed) * out_gain_ref[...] * gate[...].astype(jnp.float32)
    out = jnp.dot(
        gated.astype(jnp.bfloat16), w_out_buf[...], preferred_element_type=jnp.float32
    )
    layer_rows = (x_ref[0].astype(jnp.float32) + out).astype(jnp.bfloat16)

    rows = 16
    which_user = lax.broadcasted_iota(jnp.int32, (rows, tok), 0)
    slot = lax.broadcasted_iota(jnp.int32, (rows, tok), 1) + me * tok
    last = jnp.full((rows, tok), -1, jnp.int32)
    for u in range(USERS):
        last = jnp.where(which_user == u, starts[u] * BLK + lengths[u] - 1, last)
    picker = jnp.where(slot == last, 1.0, 0.0).astype(jnp.bfloat16)
    states = jnp.dot(picker, layer_rows, preferred_element_type=jnp.float32).astype(jnp.bfloat16)
    pltpu.make_async_copy(table_ref, table_buf.at[dp], table_sem).wait()
    for step in range(1, n_dp):
        source = (dp + step) % n_dp
        pltpu.make_async_copy(
            table_buf.at[source], table_buf.at[source], table_recv.at[source]
        ).wait()
    node_scores = lax.dot_general(
        states,
        table_buf[...].reshape(n_dp * nodes, width),
        (((1,), (1,)), ((), ())),
        preferred_element_type=jnp.float32,
    )
    pieces = [
        node_scores[u : u + 1, c * LANES : (c + 1) * LANES]
        for u in range(USERS)
        for c in range(chunks)
    ]
    spare = part_sent.shape[0] - len(pieces)
    if spare:
        pieces.append(jnp.zeros((spare, LANES), jnp.float32))
    part = jnp.concatenate(pieces, axis=0).astype(jnp.bfloat16)
    part_sent[...] = part
    part_recv[me] = part
    for step in far_first(n_seq):
        copy = remote(
            part_sent,
            part_recv.at[me],
            p_send.at[step],
            p_recv.at[me],
            {"seq": (me + step) % n_seq},
        )
        copy.start()
        waits.append(copy)

    layer_ref[0] = layer_rows

    for copy in waits:
        copy.wait_send()
    for head in range(heads):
        for core_to in range(2):
            away = me != 2 * head + core_to
            where = {"seq": 2 * head + core_to}

            @pl.when(away)
            def _():
                remote(
                    sent.at[0, head, pl.ds(core_to * half, half)],
                    query.at[me],
                    q_send.at[2 * head + core_to],
                    q_recv.at[me],
                    where,
                ).wait_send()

            @pl.when(away & ((chip == head) | (core == core_to)))
            def _():
                for which in range(2):
                    remote(
                        sent.at[which + 1, head],
                        kv.at[which, me],
                        kv_send.at[which, 2 * head + core_to],
                        kv_recv.at[which, me],
                        where,
                    ).wait_send()

    for step in far_first(n_seq):
        source = (me + step) % n_seq
        pltpu.make_async_copy(
            part_recv.at[source], part_recv.at[source], p_recv.at[source]
        ).wait()
    total = jnp.sum(part_recv[...].astype(jnp.float32), axis=0)
    users = [
        jnp.concatenate(
            [total[u * chunks + c : u * chunks + c + 1] for c in range(chunks)], axis=1
        )
        for u in range(USERS)
    ]
    users.append(jnp.zeros((rows - USERS, n_dp * nodes), jnp.float32))
    score_rows = jnp.concatenate(users, axis=0).astype(jnp.bfloat16)
    picked = jnp.dot(score_rows, onehot[...], preferred_element_type=jnp.float32)
    for u in range(USERS):
        scores_ref[u : u + 1] = picked[u : u + 1, u * per_user : (u + 1) * per_user]


def hand_over(layer_in, scores_in, layer_out, scores_out, layer_sem, scores_sem):
    layer = pltpu.make_async_copy(layer_in, layer_out, layer_sem)
    scores = pltpu.make_async_copy(scores_in, scores_out, scores_sem)
    layer.start()
    scores.start()
    layer.wait()
    scores.wait()


def body(
    n_dp,
    n_seq,
    tokens,
    in_gain,
    w_proj,
    out_gain,
    w_out,
    rab_slope,
    hist_blocks,
    hist_tail,
    node_table,
    subtree_map,
    beam_nodes,
):
    _, tok, width = tokens.shape
    heads = rab_slope.shape[0]
    head_dim = width // heads
    nodes = node_table.shape[0]
    half = tok // 2
    assert n_seq == 2 * heads and tok == BLK
    window = n_seq // 2 + 2
    part_rows = -(-USERS * n_dp * nodes // LANES // 16) * 16
    vmem = pl.BlockSpec(memory_space=pltpu.VMEM)
    smem = pl.BlockSpec(memory_space=pltpu.SMEM)
    hbm = pl.BlockSpec(memory_space=pl.ANY)
    dma = pltpu.SemaphoreType.DMA
    bf16 = jnp.bfloat16
    layer_out, scores = pl.pallas_call(
        functools.partial(layer_kernel, n_dp, n_seq),
        out_shape=(
            jax.ShapeDtypeStruct(tokens.shape, bf16),
            jax.ShapeDtypeStruct(beam_nodes.shape, jnp.float32),
        ),
        in_specs=[hbm, vmem, hbm, vmem, hbm, smem, smem, smem, hbm, smem, vmem],
        out_specs=(vmem, vmem),
        scratch_shapes=[
            pltpu.VMEM(tokens.shape, bf16),
            pltpu.VMEM((4, heads // 2, width, 2 * head_dim), bf16),
            pltpu.VMEM((width, width), bf16),
            pltpu.VMEM((n_dp, nodes, width), bf16),
            pltpu.VMEM((3, heads, tok, head_dim), bf16),
            pltpu.VMEM((tok, width), bf16),
            pltpu.VMEM((2, n_seq, tok, head_dim), bf16),
            pltpu.VMEM((n_seq + window, half, head_dim), bf16),
            pltpu.VMEM((n_seq + window, half, head_dim), jnp.float32),
            pltpu.VMEM((n_seq, half, head_dim), bf16),
            pltpu.VMEM((heads, tok, head_dim), bf16),
            pltpu.VMEM(((window + 1) * half, 2 * tok), jnp.float32),
            pltpu.VMEM((part_rows, LANES), bf16),
            pltpu.VMEM((n_seq, part_rows, LANES), bf16),
            pltpu.VMEM((n_dp * nodes, USERS * beam_nodes.shape[1]), bf16),
            dma,
            dma((4, heads // 2)),
            dma,
            dma,
            dma((n_dp,)),
            dma((n_dp,)),
            dma((2, n_seq)),
            dma((2, n_seq)),
            dma((2, heads)),
            dma((n_seq,)),
            dma((n_seq,)),
            dma((n_seq,)),
            dma((n_seq,)),
            dma((n_seq,)),
            dma((n_seq,)),
        ],
        compiler_params=pltpu.CompilerParams(
            collective_id=0, has_side_effects=True, vmem_limit_bytes=56 * 1024 * 1024
        ),
    )(
        tokens,
        in_gain.reshape(1, width),
        w_proj,
        out_gain.reshape(1, width),
        w_out,
        rab_slope,
        hist_blocks,
        hist_tail,
        node_table,
        subtree_map,
        beam_nodes,
    )
    return pl.pallas_call(
        hand_over,
        out_shape=(
            jax.ShapeDtypeStruct(layer_out.shape, bf16),
            jax.ShapeDtypeStruct(scores.shape, jnp.float32),
        ),
        in_specs=[pl.BlockSpec(memory_space=pltpu.HBM)] * 2,
        out_specs=(pl.BlockSpec(memory_space=pltpu.HBM),) * 2,
        scratch_shapes=[dma, dma],
        compiler_params=pltpu.CompilerParams(vmem_limit_bytes=56 * 1024 * 1024),
    )(layer_out, scores)


def solution(mesh):
    placed = (
        P("dp", "seq", None),
        P(),
        P(),
        P(),
        P(),
        P(),
        P("dp", None),
        P("dp", None),
        P("dp", None),
        P(),
        P("dp", "seq"),
    )
    return jax.shard_map(
        functools.partial(body, mesh.shape["dp"], mesh.shape["seq"]),
        mesh=mesh,
        in_specs=placed,
        out_specs=(P("dp", "seq", None), P("dp", "seq")),
        check_vma=False,
    )
```

```python
import functools

import jax
import jax.numpy as jnp
from jax import lax
from jax.experimental import pallas as pl
from jax.experimental.pallas import tpu as pltpu
from jax.sharding import PartitionSpec as P

BLK = 128
SUBT = 64
USERS = 3
LANES = 128
MESH = pl.DeviceIdType.MESH
OFF = -1e30


def layer_norm(rows):
    centred = rows - jnp.mean(rows, axis=-1, keepdims=True)
    spread = jnp.mean(centred * centred, axis=-1, keepdims=True)
    return centred * lax.rsqrt(spread + 1e-05)


def silu_of_half(half):
    return half + half * jnp.tanh(half)


def far_first(count):
    order = []
    for step in range(count // 2):
        for offset in (count // 2 - step, count // 2 + step):
            if 0 < offset < count and offset not in order:
                order.append(offset)
    return order


def layer_kernel(
    n_dp,
    n_seq,
    x_hbm,
    in_gain_ref,
    w_proj_ref,
    out_gain_ref,
    w_out_ref,
    slope_ref,
    blocks_ref,
    tail_ref,
    table_ref,
    map_ref,
    beam_ref,
    layer_ref,
    scores_ref,
    x_ref,
    w_buf,
    w_out_buf,
    table_buf,
    sent,
    gate,
    kv,
    query,
    result,
    mix,
    bias,
    part_sent,
    part_recv,
    onehot,
    x_sem,
    w_sem,
    w_out_sem,
    table_sem,
    table_send,
    table_recv,
    table_fwd,
    table_relay,
    kv_send,
    kv_recv,
    fwd_send,
    q_send,
    q_recv,
    r_send,
    r_recv,
    p_send,
    p_recv,
):
    tok, width = x_ref.shape[1:]
    heads, _, head_dim = mix.shape
    half = query.shape[1]
    window = bias.shape[1] // tok
    nodes = table_ref.shape[0]
    chunks = n_dp * nodes // LANES
    me = lax.axis_index("seq")
    dp = lax.axis_index("dp")
    chip, core = me // 2, me % 2
    sibling = chip * 2 + (1 - core)

    def remote(src, dst, send_sem, recv_sem, where):
        return pltpu.make_async_remote_copy(
            src_ref=src,
            dst_ref=dst,
            send_sem=send_sem,
            recv_sem=recv_sem,
            device_id=where,
            device_id_type=MESH,
        )

    x_copy = pltpu.make_async_copy(x_hbm, x_ref, x_sem)
    x_copy.start()
    order = (2, 3, 1, 0)
    w_copies = {
        part: pltpu.make_async_copy(
            w_proj_ref.at[:, pl.ds(part * width, width)], w_buf.at[part], w_sem.at[part]
        )
        for part in order
    }
    for part in order:
        w_copies[part].start()

    barrier = pltpu.get_barrier_semaphore()
    for step in range(1, n_seq):
        pl.semaphore_signal(
            barrier, inc=1, device_id={"seq": (me + step) % n_seq}, device_id_type=MESH
        )
    for step in range(1, n_dp):
        pl.semaphore_signal(
            barrier, inc=1, device_id={"dp": (dp + step) % n_dp}, device_id_type=MESH
        )

    x_copy.wait()
    x_rows = x_ref[0].astype(jnp.float32)
    normed = (layer_norm(x_rows) * in_gain_ref[...]).astype(jnp.bfloat16)

    def project(part, store):
        w_copies[part].wait()
        for piece in range(heads // 2):
            columns = pl.ds(piece * 2 * head_dim, 2 * head_dim)
            out = jnp.dot(normed, w_buf[part, :, columns], preferred_element_type=jnp.float32)
            store(piece, silu_of_half(0.5 * out).astype(jnp.bfloat16))

    def store_heads(slot):
        def store(piece, rows):
            sent[slot, 2 * piece] = rows[:, :head_dim]
            sent[slot, 2 * piece + 1] = rows[:, head_dim:]

        return store

    chip_order = far_first(heads)
    waits = []
    pl.semaphore_wait(barrier, n_seq - 1 + n_dp - 1)

    part_nodes = nodes // 2
    for step in range(1, n_dp):
        mine = pl.ds(core * part_nodes, part_nodes)
        copy = remote(
            table_ref.at[mine],
            table_buf.at[dp, mine],
            table_send.at[step],
            table_recv.at[dp],
            {"dp": (dp + step) % n_dp},
        )
        copy.start()
        waits.append(copy)
    pltpu.make_async_copy(table_ref, table_buf.at[dp], table_sem).start()
    for which in range(2):
        slot = which + 1
        project(slot + 1, store_heads(slot))
        for step in chip_order:
            head = (chip + step) % heads
            copy = remote(
                sent.at[slot, head],
                kv.at[which, me],
                kv_send.at[which, step],
                kv_recv.at[which, me],
                {"seq": head * 2 + core},
            )
            copy.start()
            waits.append(copy)
        copy = remote(
            sent.at[slot, chip],
            kv.at[which, me],
            kv_send.at[which, 0],
            kv_recv.at[which, me],
            {"seq": sibling},
        )
        copy.start()
        waits.append(copy)
        pltpu.make_async_copy(
            sent.at[slot, chip], kv.at[which, me], kv_recv.at[which, me]
        ).start()

    project(1, store_heads(0))
    for step in chip_order:
        head = (chip + step) % heads
        for part in range(2):
            copy = remote(
                sent.at[0, head, pl.ds(part * half, half)],
                query.at[me],
                q_send.at[2 * step + part],
                q_recv.at[me],
                {"seq": head * 2 + part},
            )
            copy.start()
            waits.append(copy)
    copy = remote(
        sent.at[0, chip, pl.ds((1 - core) * half, half)],
        query.at[me],
        q_send.at[0],
        q_recv.at[me],
        {"seq": sibling},
    )
    copy.start()
    waits.append(copy)
    pltpu.make_async_copy(
        sent.at[0, chip, pl.ds(core * half, half)], query.at[me], q_recv.at[me]
    ).start()

    w_out_copy = pltpu.make_async_copy(w_out_ref, w_out_buf, w_out_sem)
    w_out_copy.start()

    def store_gate(piece, rows):
        gate[:, pl.ds(piece * 2 * head_dim, 2 * head_dim)] = rows

    project(0, store_gate)

    row = lax.broadcasted_iota(jnp.int32, bias.shape, 0)
    column = lax.broadcasted_iota(jnp.int32, bias.shape, 1)
    gap = (window - 1) * tok + core * half + row - column
    slope = slope_ref[chip]
    logs = jnp.log(1.0 + jnp.maximum(gap, 0).astype(jnp.float32))
    bias[...] = jnp.where(gap >= 0, (0.5 * slope) * logs, OFF)

    beams = beam_ref[...]
    subtree = beams >> 6
    base = jnp.zeros_like(beams)
    for index in range(map_ref.shape[0]):
        base = jnp.where(subtree == index, map_ref[index], base)
    stored = base * SUBT + (beams & (SUBT - 1))
    per_user = beams.shape[1]
    stored_row = jnp.concatenate([stored[u : u + 1] for u in range(USERS)], axis=1)
    node = lax.broadcasted_iota(jnp.int32, onehot.shape, 0)
    onehot[...] = jnp.where(node == stored_row, 1.0, 0.0).astype(jnp.bfloat16)

    starts = [0, blocks_ref[0, 0], blocks_ref[0, 0] + blocks_ref[0, 1]]
    lengths = [(blocks_ref[0, u] - 1) * BLK + tail_ref[0, u] for u in range(USERS)]

    def attend(block):
        pltpu.make_async_copy(query.at[block], query.at[block], q_recv.at[block]).wait()
        count = min(block + 1, window)
        low = block + 1 - count
        keys = kv[0, low : block + 1].reshape(count * tok, head_dim)
        values = kv[1, low : block + 1].reshape(count * tok, head_dim)
        first = jnp.where(block >= starts[1], starts[1], 0)
        length = jnp.where(block >= starts[1], lengths[1], lengths[0])
        first = jnp.where(block >= starts[2], starts[2], first)
        length = jnp.where(block >= starts[2], lengths[2], length)
        column = lax.broadcasted_iota(jnp.int32, (1, count * tok), 1) + low * tok
        seen = jnp.where(column >= first * tok, 0.0, OFF)
        scores = lax.dot_general(
            query[block], keys, (((1,), (1,)), ((), ())), preferred_element_type=jnp.float32
        )
        halves = scores * (0.5 * head_dim ** (-0.5)) + bias[:, (window - count) * tok :] + seen
        weights = silu_of_half(halves).astype(jnp.bfloat16)
        out = jnp.dot(weights, values, preferred_element_type=jnp.float32)
        row = lax.broadcasted_iota(jnp.int32, (half, head_dim), 0)
        live = (block - first) * tok + core * half + row < length
        result[block] = jnp.where(live, out, 0.0).astype(jnp.bfloat16)
        landing = mix.at[chip, pl.ds(core * half, half)]

        @pl.when(me != block)
        def _():
            remote(
                result.at[block], landing, r_send.at[block], r_recv.at[me], {"seq": block}
            ).start()

        @pl.when(me == block)
        def _():
            pltpu.make_async_copy(result.at[block], landing, r_recv.at[me]).start()

    def attend_chip(other):
        for which in range(2):
            relayed = 2 * other + (1 - core)
            pltpu.make_async_copy(
                kv.at[which, relayed], kv.at[which, relayed], kv_recv.at[which, relayed]
            ).wait()
        for block in (2 * other, 2 * other + 1):
            attend(block)

    for other in range(heads):
        direct = 2 * other + core
        for which in range(2):
            landed = kv.at[which, direct]
            pltpu.make_async_copy(landed, landed, kv_recv.at[which, direct]).wait()

            @pl.when(other != chip)
            def _():
                remote(
                    landed,
                    landed,
                    fwd_send.at[which, other],
                    kv_recv.at[which, direct],
                    {"seq": sibling},
                ).start()

        if other > 0:
            attend_chip(other - 1)
    for step in range(1, n_dp):
        source = (dp + step) % n_dp
        came = table_buf.at[source, pl.ds(core * part_nodes, part_nodes)]
        pltpu.make_async_copy(came, came, table_recv.at[source]).wait()
        copy = remote(came, came, table_fwd.at[step], table_relay.at[source], {"seq": sibling})
        copy.start()
        waits.append(copy)
    attend_chip(heads - 1)

    w_out_copy.wait()
    for source in range(n_seq):
        landing = mix.at[source // 2, pl.ds((source % 2) * half, half)]
        pltpu.make_async_copy(landing, landing, r_recv.at[source]).wait()
    mixed = jnp.concatenate([mix[head] for head in range(heads)], axis=1).astype(jnp.float32)
    gated = layer_norm(mixed) * out_gain_ref[...] * gate[...].astype(jnp.float32)
    out = jnp.dot(
        gated.astype(jnp.bfloat16), w_out_buf[...], preferred_element_type=jnp.float32
    )
    layer_rows = (x_ref[0].astype(jnp.float32) + out).astype(jnp.bfloat16)

    rows = 16
    which_user = lax.broadcasted_iota(jnp.int32, (rows, tok), 0)
    slot = lax.broadcasted_iota(jnp.int32, (rows, tok), 1) + me * tok
    last = jnp.full((rows, tok), -1, jnp.int32)
    for u in range(USERS):
        last = jnp.where(which_user == u, starts[u] * BLK + lengths[u] - 1, last)
    picker = jnp.where(slot == last, 1.0, 0.0).astype(jnp.bfloat16)
    states = jnp.dot(picker, layer_rows, preferred_element_type=jnp.float32).astype(jnp.bfloat16)
    pltpu.make_async_copy(table_ref, table_buf.at[dp], table_sem).wait()
    for step in range(1, n_dp):
        source = (dp + step) % n_dp
        came = table_buf.at[source, pl.ds((1 - core) * part_nodes, part_nodes)]
        pltpu.make_async_copy(came, came, table_relay.at[source]).wait()
    node_scores = lax.dot_general(
        states,
        table_buf[...].reshape(n_dp * nodes, width),
        (((1,), (1,)), ((), ())),
        preferred_element_type=jnp.float32,
    )
    pieces = [
        node_scores[u : u + 1, c * LANES : (c + 1) * LANES]
        for u in range(USERS)
        for c in range(chunks)
    ]
    spare = part_sent.shape[0] - len(pieces)
    if spare:
        pieces.append(jnp.zeros((spare, LANES), jnp.float32))
    part = jnp.concatenate(pieces, axis=0).astype(jnp.bfloat16)
    part_sent[...] = part
    part_recv[me] = part
    for step in far_first(n_seq):
        copy = remote(
            part_sent,
            part_recv.at[me],
            p_send.at[step],
            p_recv.at[me],
            {"seq": (me + step) % n_seq},
        )
        copy.start()
        waits.append(copy)

    layer_ref[0] = layer_rows

    for copy in waits:
        copy.wait_send()
    for other in range(heads):
        direct = 2 * other + core

        @pl.when(other != chip)
        def _():
            for which in range(2):
                remote(
                    kv.at[which, direct],
                    kv.at[which, direct],
                    fwd_send.at[which, other],
                    kv_recv.at[which, direct],
                    {"seq": sibling},
                ).wait_send()

    for block in range(n_seq):

        @pl.when(me != block)
        def _():
            remote(
                result.at[block],
                mix.at[chip, pl.ds(core * half, half)],
                r_send.at[block],
                r_recv.at[me],
                {"seq": block},
            ).wait_send()

    for step in far_first(n_seq):
        source = (me + step) % n_seq
        pltpu.make_async_copy(
            part_recv.at[source], part_recv.at[source], p_recv.at[source]
        ).wait()
    total = jnp.sum(part_recv[...].astype(jnp.float32), axis=0)
    users = [
        jnp.concatenate(
            [total[u * chunks + c : u * chunks + c + 1] for c in range(chunks)], axis=1
        )
        for u in range(USERS)
    ]
    users.append(jnp.zeros((rows - USERS, n_dp * nodes), jnp.float32))
    score_rows = jnp.concatenate(users, axis=0).astype(jnp.bfloat16)
    picked = jnp.dot(score_rows, onehot[...], preferred_element_type=jnp.float32)
    for u in range(USERS):
        scores_ref[u : u + 1] = picked[u : u + 1, u * per_user : (u + 1) * per_user]


def hand_over(layer_in, scores_in, layer_out, scores_out, layer_sem, scores_sem):
    layer = pltpu.make_async_copy(layer_in, layer_out, layer_sem)
    scores = pltpu.make_async_copy(scores_in, scores_out, scores_sem)
    layer.start()
    scores.start()
    layer.wait()
    scores.wait()


def body(
    n_dp,
    n_seq,
    tokens,
    in_gain,
    w_proj,
    out_gain,
    w_out,
    rab_slope,
    hist_blocks,
    hist_tail,
    node_table,
    subtree_map,
    beam_nodes,
):
    _, tok, width = tokens.shape
    heads = rab_slope.shape[0]
    head_dim = width // heads
    nodes = node_table.shape[0]
    half = tok // 2
    assert n_seq == 2 * heads and tok == BLK
    window = n_seq // 2 + 2
    part_rows = -(-USERS * n_dp * nodes // LANES // 16) * 16
    vmem = pl.BlockSpec(memory_space=pltpu.VMEM)
    smem = pl.BlockSpec(memory_space=pltpu.SMEM)
    hbm = pl.BlockSpec(memory_space=pl.ANY)
    dma = pltpu.SemaphoreType.DMA
    bf16 = jnp.bfloat16
    layer_out, scores = pl.pallas_call(
        functools.partial(layer_kernel, n_dp, n_seq),
        out_shape=(
            jax.ShapeDtypeStruct(tokens.shape, bf16),
            jax.ShapeDtypeStruct(beam_nodes.shape, jnp.float32),
        ),
        in_specs=[hbm, vmem, hbm, vmem, hbm, smem, smem, smem, hbm, smem, vmem],
        out_specs=(vmem, vmem),
        scratch_shapes=[
            pltpu.VMEM(tokens.shape, bf16),
            pltpu.VMEM((4, width, width), bf16),
            pltpu.VMEM((width, width), bf16),
            pltpu.VMEM((n_dp, nodes, width), bf16),
            pltpu.VMEM((3, heads, tok, head_dim), bf16),
            pltpu.VMEM((tok, width), bf16),
            pltpu.VMEM((2, n_seq, tok, head_dim), bf16),
            pltpu.VMEM((n_seq, half, head_dim), bf16),
            pltpu.VMEM((n_seq, half, head_dim), bf16),
            pltpu.VMEM((heads, tok, head_dim), bf16),
            pltpu.VMEM((half, window * tok), jnp.float32),
            pltpu.VMEM((part_rows, LANES), bf16),
            pltpu.VMEM((n_seq, part_rows, LANES), bf16),
            pltpu.VMEM((n_dp * nodes, USERS * beam_nodes.shape[1]), bf16),
            dma,
            dma((4,)),
            dma,
            dma,
            dma((n_dp,)),
            dma((n_dp,)),
            dma((n_dp,)),
            dma((n_dp,)),
            dma((2, heads)),
            dma((2, n_seq)),
            dma((2, heads)),
            dma((n_seq,)),
            dma((n_seq,)),
            dma((n_seq,)),
            dma((n_seq,)),
            dma((n_seq,)),
            dma((n_seq,)),
        ],
        compiler_params=pltpu.CompilerParams(
            collective_id=0, has_side_effects=True, vmem_limit_bytes=56 * 1024 * 1024
        ),
    )(
        tokens,
        in_gain.reshape(1, width),
        w_proj,
        out_gain.reshape(1, width),
        w_out,
        rab_slope,
        hist_blocks,
        hist_tail,
        node_table,
        subtree_map,
        beam_nodes,
    )
    return pl.pallas_call(
        hand_over,
        out_shape=(
            jax.ShapeDtypeStruct(layer_out.shape, bf16),
            jax.ShapeDtypeStruct(scores.shape, jnp.float32),
        ),
        in_specs=[vmem, vmem],
        out_specs=(hbm, hbm),
        scratch_shapes=[dma, dma],
    )(layer_out, scores)


def solution(mesh):
    placed = (
        P("dp", "seq", None),
        P(),
        P(),
        P(),
        P(),
        P(),
        P("dp", None),
        P("dp", None),
        P("dp", None),
        P(),
        P("dp", "seq"),
    )
    return jax.shard_map(
        functools.partial(body, mesh.shape["dp"], mesh.shape["seq"]),
        mesh=mesh,
        in_specs=placed,
        out_specs=(P("dp", "seq", None), P("dp", "seq")),
        check_vma=False,
    )
```

```python
import functools

import jax
import jax.numpy as jnp
from jax import lax
from jax.experimental import pallas as pl
from jax.experimental.pallas import tpu as pltpu
from jax.sharding import PartitionSpec as P

BLK = 128
SUBT = 64
USERS = 3
LANES = 128
MESH = pl.DeviceIdType.MESH
OFF = -1e30


def layer_norm(rows):
    centred = rows - jnp.mean(rows, axis=-1, keepdims=True)
    spread = jnp.mean(centred * centred, axis=-1, keepdims=True)
    return centred * lax.rsqrt(spread + 1e-05)


def silu_of_half(half):
    return half + half * jnp.tanh(half)


def far_first(count):
    order = []
    for step in range(count // 2):
        for offset in (count // 2 - step, count // 2 + step):
            if 0 < offset < count and offset not in order:
                order.append(offset)
    return order


def layer_kernel(
    n_dp,
    n_seq,
    x_hbm,
    in_gain_ref,
    w_proj_ref,
    out_gain_ref,
    w_out_ref,
    slope_ref,
    blocks_ref,
    tail_ref,
    table_ref,
    map_ref,
    beam_ref,
    layer_ref,
    scores_ref,
    x_ref,
    w_buf,
    w_out_buf,
    table_buf,
    sent,
    gate,
    kv,
    query,
    result,
    mix,
    mix_low,
    bias,
    part_sent,
    part_recv,
    onehot,
    x_sem,
    w_sem,
    w_out_sem,
    table_sem,
    table_send,
    table_recv,
    table_fwd,
    table_relay,
    kv_send,
    kv_recv,
    q_send,
    cross_send,
    q_recv,
    r_send,
    r_recv,
    r_low_recv,
    p_send,
    p_recv,
):
    tok, width = x_ref.shape[1:]
    heads, _, head_dim = mix.shape
    nodes = table_ref.shape[0]
    chunks = n_dp * nodes // LANES
    me = lax.axis_index("seq")
    dp = lax.axis_index("dp")
    side, mine = me // heads, me % heads
    base = side * heads
    core = me % 2
    sibling = me + 1 - 2 * core

    def remote(src, dst, send_sem, recv_sem, where):
        return pltpu.make_async_remote_copy(
            src_ref=src,
            dst_ref=dst,
            send_sem=send_sem,
            recv_sem=recv_sem,
            device_id=where,
            device_id_type=MESH,
        )

    x_copy = pltpu.make_async_copy(x_hbm, x_ref, x_sem)
    x_copy.start()
    order = (1, 2, 3, 0)
    w_copies = {
        part: pltpu.make_async_copy(
            w_proj_ref.at[:, pl.ds(part * width, width)], w_buf.at[part], w_sem.at[part]
        )
        for part in order
    }
    for part in order:
        w_copies[part].start()

    barrier = pltpu.get_barrier_semaphore()
    for step in range(1, n_seq):
        pl.semaphore_signal(
            barrier, inc=1, device_id={"seq": (me + step) % n_seq}, device_id_type=MESH
        )
    for step in range(1, n_dp):
        pl.semaphore_signal(
            barrier, inc=1, device_id={"dp": (dp + step) % n_dp}, device_id_type=MESH
        )

    x_copy.wait()
    x_rows = x_ref[0].astype(jnp.float32)
    normed = (layer_norm(x_rows) * in_gain_ref[...]).astype(jnp.bfloat16)

    def project(part, store):
        w_copies[part].wait()
        for piece in range(heads // 2):
            columns = pl.ds(piece * 2 * head_dim, 2 * head_dim)
            out = jnp.dot(normed, w_buf[part, :, columns], preferred_element_type=jnp.float32)
            store(piece, silu_of_half(0.5 * out).astype(jnp.bfloat16))

    def store_heads(slot):
        def store(piece, rows):
            sent[slot, 2 * piece] = rows[:, :head_dim]
            sent[slot, 2 * piece + 1] = rows[:, head_dim:]

        return store

    waits = []
    for slot, landing, send_sem, recv_sem in (
        (0, query.at[me], q_send, q_recv.at[me]),
        (1, kv.at[0, mine], kv_send.at[0], kv_recv.at[0, mine]),
        (2, kv.at[1, mine], kv_send.at[1], kv_recv.at[1, mine]),
    ):
        project(slot + 1, store_heads(slot))
        if slot == 0:
            pl.semaphore_wait(barrier, n_seq - 1 + n_dp - 1)
        for step in range(heads):
            head = (mine + step) % heads
            if slot == 0:

                @pl.when(side == 1)
                def _():
                    remote(
                        sent.at[0, head],
                        query.at[me],
                        cross_send.at[step],
                        q_recv.at[me],
                        {"seq": head},
                    ).start()

            if step == 0:
                pltpu.make_async_copy(sent.at[slot, head], landing, recv_sem).start()
            else:
                copy = remote(
                    sent.at[slot, head], landing, send_sem.at[step], recv_sem, {"seq": base + head}
                )
                copy.start()
                waits.append(copy)

    part_nodes = nodes // 2
    for step in range(1, n_dp):
        own_rows = pl.ds(core * part_nodes, part_nodes)
        copy = remote(
            table_ref.at[own_rows],
            table_buf.at[dp, own_rows],
            table_send.at[step],
            table_recv.at[dp],
            {"dp": (dp + step) % n_dp},
        )
        copy.start()
        waits.append(copy)
    pltpu.make_async_copy(table_ref, table_buf.at[dp], table_sem).start()
    w_out_copy = pltpu.make_async_copy(w_out_ref, w_out_buf, w_out_sem)
    w_out_copy.start()

    def store_gate(piece, rows):
        gate[:, pl.ds(piece * 2 * head_dim, 2 * head_dim)] = rows

    project(0, store_gate)

    row = lax.broadcasted_iota(jnp.int32, bias.shape, 0)
    column = lax.broadcasted_iota(jnp.int32, bias.shape, 1)
    gap = (n_seq - 1) * tok + row - column
    slope = slope_ref[mine]
    logs = jnp.log(1.0 + jnp.maximum(gap, 0).astype(jnp.float32))
    bias[...] = jnp.where(gap >= 0, (0.5 * slope) * logs, OFF)

    @pl.when(side == 0)
    def _():
        mix_low[...] = jnp.zeros_like(mix_low)

    beams = beam_ref[...]
    subtree = beams >> 6
    found = jnp.zeros_like(beams)
    for index in range(map_ref.shape[0]):
        found = jnp.where(subtree == index, map_ref[index], found)
    stored = found * SUBT + (beams & (SUBT - 1))
    per_user = beams.shape[1]
    stored_row = jnp.concatenate([stored[u : u + 1] for u in range(USERS)], axis=1)
    node = lax.broadcasted_iota(jnp.int32, onehot.shape, 0)
    onehot[...] = jnp.where(node == stored_row, 1.0, 0.0).astype(jnp.bfloat16)

    starts = [0, blocks_ref[0, 0], blocks_ref[0, 0] + blocks_ref[0, 1]]
    lengths = [(blocks_ref[0, u] - 1) * BLK + tail_ref[0, u] for u in range(USERS)]

    def landed(ref, sem):
        pltpu.make_async_copy(ref, ref, sem).wait()

    def attend(block, first_key, key_rows, value_rows, bias_rows):
        first = jnp.where(block >= starts[1], starts[1], 0)
        length = jnp.where(block >= starts[1], lengths[1], lengths[0])
        first = jnp.where(block >= starts[2], starts[2], first)
        length = jnp.where(block >= starts[2], lengths[2], length)
        column = lax.broadcasted_iota(jnp.int32, (1, key_rows.shape[0]), 1) + first_key * tok
        seen = jnp.where(column >= first * tok, 0.0, OFF)
        scores = lax.dot_general(
            query[block], key_rows, (((1,), (1,)), ((), ())), preferred_element_type=jnp.float32
        )
        halves = scores * (0.5 * head_dim ** (-0.5)) + bias_rows + seen
        weights = silu_of_half(halves).astype(jnp.bfloat16)
        out = jnp.dot(weights, value_rows, preferred_element_type=jnp.float32)
        row = lax.broadcasted_iota(jnp.int32, (tok, head_dim), 0)
        live = (block - first) * tok + row < length
        return jnp.where(live, out, 0.0).astype(jnp.bfloat16)

    def key_values(which, count):
        return kv[which, 0:count].reshape(count * tok, head_dim)

    for place in range(heads):
        block = base + place
        landed(query.at[block], q_recv.at[block])
        for which in range(2):
            landed(kv.at[which, place], kv_recv.at[which, place])
        count = place + 1
        result[place] = attend(
            block,
            base,
            key_values(0, count),
            key_values(1, count),
            bias[:, (n_seq - count) * tok :],
        )

        @pl.when(mine != place)
        def _():
            remote(
                result.at[place], mix.at[mine], r_send.at[place], r_recv.at[mine], {"seq": block}
            ).start()

        @pl.when(mine == place)
        def _():
            pltpu.make_async_copy(result.at[place], mix.at[mine], r_recv.at[mine]).start()

    for step in range(1, n_dp):
        source = (dp + step) % n_dp
        came = table_buf.at[source, pl.ds(core * part_nodes, part_nodes)]
        landed(came, table_recv.at[source])
        copy = remote(came, came, table_fwd.at[step], table_relay.at[source], {"seq": sibling})
        copy.start()
        waits.append(copy)

    @pl.when(side == 0)
    def _():
        copies = []
        for step in range(heads):
            block = heads + (mine + heads - step) % heads
            landed(query.at[block], q_recv.at[block])
            offset = pl.multiple_of((n_seq - 1 - block) * tok, tok)
            result[heads + step] = attend(
                block,
                0,
                key_values(0, heads),
                key_values(1, heads),
                bias[:, pl.ds(offset, heads * tok)],
            )
            copy = remote(
                result.at[heads + step],
                mix_low.at[mine],
                r_send.at[heads + step],
                r_low_recv.at[mine],
                {"seq": block},
            )
            copy.start()
            copies.append(copy)
        for copy in copies:
            copy.wait_send()

    w_out_copy.wait()
    for source in range(heads):
        landed(mix.at[source], r_recv.at[source])

    @pl.when(side == 1)
    def _():
        for source in range(heads):
            landed(mix_low.at[source], r_low_recv.at[source])

    mixed = jnp.concatenate(
        [
            mix[head].astype(jnp.float32) + mix_low[head].astype(jnp.float32)
            for head in range(heads)
        ],
        axis=1,
    )
    gated = layer_norm(mixed) * out_gain_ref[...] * gate[...].astype(jnp.float32)
    out = jnp.dot(
        gated.astype(jnp.bfloat16), w_out_buf[...], preferred_element_type=jnp.float32
    )
    layer_rows = (x_ref[0].astype(jnp.float32) + out).astype(jnp.bfloat16)

    rows = 16
    which_user = lax.broadcasted_iota(jnp.int32, (rows, tok), 0)
    slot = lax.broadcasted_iota(jnp.int32, (rows, tok), 1) + me * tok
    last = jnp.full((rows, tok), -1, jnp.int32)
    for u in range(USERS):
        last = jnp.where(which_user == u, starts[u] * BLK + lengths[u] - 1, last)
    picker = jnp.where(slot == last, 1.0, 0.0).astype(jnp.bfloat16)
    states = jnp.dot(picker, layer_rows, preferred_element_type=jnp.float32).astype(jnp.bfloat16)
    pltpu.make_async_copy(table_ref, table_buf.at[dp], table_sem).wait()
    for step in range(1, n_dp):
        source = (dp + step) % n_dp
        came = table_buf.at[source, pl.ds((1 - core) * part_nodes, part_nodes)]
        pltpu.make_async_copy(came, came, table_relay.at[source]).wait()
    node_scores = lax.dot_general(
        states,
        table_buf[...].reshape(n_dp * nodes, width),
        (((1,), (1,)), ((), ())),
        preferred_element_type=jnp.float32,
    )
    pieces = [
        node_scores[u : u + 1, c * LANES : (c + 1) * LANES]
        for u in range(USERS)
        for c in range(chunks)
    ]
    spare = part_sent.shape[0] - len(pieces)
    if spare:
        pieces.append(jnp.zeros((spare, LANES), jnp.float32))
    part = jnp.concatenate(pieces, axis=0).astype(jnp.bfloat16)
    part_sent[...] = part
    part_recv[me] = part
    for step in far_first(n_seq):
        copy = remote(
            part_sent,
            part_recv.at[me],
            p_send.at[step],
            p_recv.at[me],
            {"seq": (me + step) % n_seq},
        )
        copy.start()
        waits.append(copy)

    layer_ref[0] = layer_rows

    for copy in waits:
        copy.wait_send()
    @pl.when(side == 1)
    def _():
        for step in range(heads):
            head = (mine + step) % heads
            remote(
                sent.at[0, head], query.at[me], cross_send.at[step], q_recv.at[me], {"seq": head}
            ).wait_send()

    for place in range(heads):

        @pl.when(mine != place)
        def _():
            remote(
                result.at[place],
                mix.at[mine],
                r_send.at[place],
                r_recv.at[mine],
                {"seq": base + place},
            ).wait_send()

    for step in far_first(n_seq):
        source = (me + step) % n_seq
        pltpu.make_async_copy(
            part_recv.at[source], part_recv.at[source], p_recv.at[source]
        ).wait()
    total = jnp.sum(part_recv[...].astype(jnp.float32), axis=0)
    users = [
        jnp.concatenate(
            [total[u * chunks + c : u * chunks + c + 1] for c in range(chunks)], axis=1
        )
        for u in range(USERS)
    ]
    users.append(jnp.zeros((rows - USERS, n_dp * nodes), jnp.float32))
    score_rows = jnp.concatenate(users, axis=0).astype(jnp.bfloat16)
    picked = jnp.dot(score_rows, onehot[...], preferred_element_type=jnp.float32)
    for u in range(USERS):
        scores_ref[u : u + 1] = picked[u : u + 1, u * per_user : (u + 1) * per_user]


def hand_over(layer_in, scores_in, layer_out, scores_out, layer_sem, scores_sem):
    layer = pltpu.make_async_copy(layer_in, layer_out, layer_sem)
    scores = pltpu.make_async_copy(scores_in, scores_out, scores_sem)
    layer.start()
    scores.start()
    layer.wait()
    scores.wait()


def body(
    n_dp,
    n_seq,
    tokens,
    in_gain,
    w_proj,
    out_gain,
    w_out,
    rab_slope,
    hist_blocks,
    hist_tail,
    node_table,
    subtree_map,
    beam_nodes,
):
    _, tok, width = tokens.shape
    heads = rab_slope.shape[0]
    head_dim = width // heads
    nodes = node_table.shape[0]
    assert n_seq == 2 * heads and tok == BLK
    part_rows = -(-USERS * n_dp * nodes // LANES // 16) * 16
    vmem = pl.BlockSpec(memory_space=pltpu.VMEM)
    smem = pl.BlockSpec(memory_space=pltpu.SMEM)
    hbm = pl.BlockSpec(memory_space=pl.ANY)
    dma = pltpu.SemaphoreType.DMA
    bf16 = jnp.bfloat16
    layer_out, scores = pl.pallas_call(
        functools.partial(layer_kernel, n_dp, n_seq),
        out_shape=(
            jax.ShapeDtypeStruct(tokens.shape, bf16),
            jax.ShapeDtypeStruct(beam_nodes.shape, jnp.float32),
        ),
        in_specs=[hbm, vmem, hbm, vmem, hbm, smem, smem, smem, hbm, smem, vmem],
        out_specs=(vmem, vmem),
        scratch_shapes=[
            pltpu.VMEM(tokens.shape, bf16),
            pltpu.VMEM((4, width, width), bf16),
            pltpu.VMEM((width, width), bf16),
            pltpu.VMEM((n_dp, nodes, width), bf16),
            pltpu.VMEM((3, heads, tok, head_dim), bf16),
            pltpu.VMEM((tok, width), bf16),
            pltpu.VMEM((2, heads, tok, head_dim), bf16),
            pltpu.VMEM((n_seq, tok, head_dim), bf16),
            pltpu.VMEM((n_seq, tok, head_dim), bf16),
            pltpu.VMEM((heads, tok, head_dim), bf16),
            pltpu.VMEM((heads, tok, head_dim), bf16),
            pltpu.VMEM((tok, n_seq * tok), jnp.float32),
            pltpu.VMEM((part_rows, LANES), bf16),
            pltpu.VMEM((n_seq, part_rows, LANES), bf16),
            pltpu.VMEM((n_dp * nodes, USERS * beam_nodes.shape[1]), bf16),
            dma,
            dma((4,)),
            dma,
            dma,
            dma((n_dp,)),
            dma((n_dp,)),
            dma((n_dp,)),
            dma((n_dp,)),
            dma((2, heads)),
            dma((2, heads)),
            dma((heads,)),
            dma((heads,)),
            dma((n_seq,)),
            dma((n_seq,)),
            dma((heads,)),
            dma((heads,)),
            dma((n_seq,)),
            dma((n_seq,)),
        ],
        compiler_params=pltpu.CompilerParams(
            collective_id=0, has_side_effects=True, vmem_limit_bytes=56 * 1024 * 1024
        ),
    )(
        tokens,
        in_gain.reshape(1, width),
        w_proj,
        out_gain.reshape(1, width),
        w_out,
        rab_slope,
        hist_blocks,
        hist_tail,
        node_table,
        subtree_map,
        beam_nodes,
    )
    return pl.pallas_call(
        hand_over,
        out_shape=(
            jax.ShapeDtypeStruct(layer_out.shape, bf16),
            jax.ShapeDtypeStruct(scores.shape, jnp.float32),
        ),
        in_specs=[vmem, vmem],
        out_specs=(hbm, hbm),
        scratch_shapes=[dma, dma],
    )(layer_out, scores)


def solution(mesh):
    placed = (
        P("dp", "seq", None),
        P(),
        P(),
        P(),
        P(),
        P(),
        P("dp", None),
        P("dp", None),
        P("dp", None),
        P(),
        P("dp", "seq"),
    )
    return jax.shard_map(
        functools.partial(body, mesh.shape["dp"], mesh.shape["seq"]),
        mesh=mesh,
        in_specs=placed,
        out_specs=(P("dp", "seq", None), P("dp", "seq")),
        check_vma=False,
    )
```

```python
import functools

import jax
import jax.numpy as jnp
from jax import lax
from jax.experimental import pallas as pl
from jax.experimental.pallas import tpu as pltpu
from jax.sharding import PartitionSpec as P

BLK = 128
SUBT = 64
USERS = 3
LANES = 128
MESH = pl.DeviceIdType.MESH
OFF = -1e30


def layer_norm(rows):
    centred = rows - jnp.mean(rows, axis=-1, keepdims=True)
    spread = jnp.mean(centred * centred, axis=-1, keepdims=True)
    return centred * lax.rsqrt(spread + 1e-05)


def silu_of_half(half):
    return half + half * jnp.tanh(half)


def far_first(count):
    order = []
    for step in range(count // 2):
        for offset in (count // 2 - step, count // 2 + step):
            if 0 < offset < count and offset not in order:
                order.append(offset)
    return order


def layer_kernel(
    n_dp,
    n_seq,
    x_hbm,
    in_gain_ref,
    w_proj_ref,
    out_gain_ref,
    w_out_ref,
    slope_ref,
    blocks_ref,
    tail_ref,
    table_ref,
    map_ref,
    beam_ref,
    layer_ref,
    scores_ref,
    x_ref,
    w_buf,
    w_out_buf,
    table_buf,
    sent,
    gate,
    kv,
    query,
    result,
    mix,
    mix_low,
    bias,
    part_sent,
    part_recv,
    onehot,
    x_sem,
    w_sem,
    w_out_sem,
    table_sem,
    table_send,
    table_recv,
    table_fwd,
    table_relay,
    kv_send,
    kv_recv,
    q_send,
    cross_send,
    q_recv,
    r_send,
    r_recv,
    r_low_recv,
    p_send,
    p_recv,
):
    tok, width = x_ref.shape[1:]
    heads, _, head_dim = mix.shape
    nodes = table_ref.shape[0]
    chunks = n_dp * nodes // LANES
    me = lax.axis_index("seq")
    dp = lax.axis_index("dp")
    side, mine = me // heads, me % heads
    base = side * heads
    window = heads + 2
    core = me % 2
    sibling = me + 1 - 2 * core

    def remote(src, dst, send_sem, recv_sem, where):
        return pltpu.make_async_remote_copy(
            src_ref=src,
            dst_ref=dst,
            send_sem=send_sem,
            recv_sem=recv_sem,
            device_id=where,
            device_id_type=MESH,
        )

    x_copy = pltpu.make_async_copy(x_hbm, x_ref, x_sem)
    x_copy.start()
    order = (1, 2, 3, 0)
    w_copies = {
        part: pltpu.make_async_copy(
            w_proj_ref.at[:, pl.ds(part * width, width)], w_buf.at[part], w_sem.at[part]
        )
        for part in order
    }
    for part in order:
        w_copies[part].start()

    barrier = pltpu.get_barrier_semaphore()
    for step in range(1, n_seq):
        pl.semaphore_signal(
            barrier, inc=1, device_id={"seq": (me + step) % n_seq}, device_id_type=MESH
        )
    for step in range(1, n_dp):
        pl.semaphore_signal(
            barrier, inc=1, device_id={"dp": (dp + step) % n_dp}, device_id_type=MESH
        )

    x_copy.wait()
    x_rows = x_ref[0].astype(jnp.float32)
    normed = (layer_norm(x_rows) * in_gain_ref[...]).astype(jnp.bfloat16)

    def project(part, store):
        w_copies[part].wait()
        for piece in range(heads // 2):
            columns = pl.ds(piece * 2 * head_dim, 2 * head_dim)
            out = jnp.dot(normed, w_buf[part, :, columns], preferred_element_type=jnp.float32)
            rows = silu_of_half(0.5 * out)
            if part == 1:
                rows = rows * (0.5 * head_dim ** (-0.5))
            store(piece, rows.astype(jnp.bfloat16))

    def store_heads(slot):
        def store(piece, rows):
            sent[slot, 2 * piece] = rows[:, :head_dim]
            sent[slot, 2 * piece + 1] = rows[:, head_dim:]

        return store

    waits = []
    for slot, landing, send_sem, recv_sem in (
        (0, query.at[me], q_send, q_recv.at[me]),
        (1, kv.at[0, mine], kv_send.at[0], kv_recv.at[0, mine]),
        (2, kv.at[1, mine], kv_send.at[1], kv_recv.at[1, mine]),
    ):
        project(slot + 1, store_heads(slot))
        if slot == 0:
            pl.semaphore_wait(barrier, n_seq - 1 + n_dp - 1)
        for step in range(heads):
            head = (mine + step) % heads
            if slot == 0:

                @pl.when(side == 1)
                def _():
                    remote(
                        sent.at[0, head],
                        query.at[me],
                        cross_send.at[step],
                        q_recv.at[me],
                        {"seq": head},
                    ).start()

            if step == 0:
                pltpu.make_async_copy(sent.at[slot, head], landing, recv_sem).start()
            else:
                copy = remote(
                    sent.at[slot, head], landing, send_sem.at[step], recv_sem, {"seq": base + head}
                )
                copy.start()
                waits.append(copy)

    part_nodes = nodes // 2
    for step in range(1, n_dp):
        own_rows = pl.ds(core * part_nodes, part_nodes)
        copy = remote(
            table_ref.at[own_rows],
            table_buf.at[dp, own_rows],
            table_send.at[step],
            table_recv.at[dp],
            {"dp": (dp + step) % n_dp},
        )
        copy.start()
        waits.append(copy)
    pltpu.make_async_copy(table_ref, table_buf.at[dp], table_sem).start()
    w_out_copy = pltpu.make_async_copy(w_out_ref, w_out_buf, w_out_sem)
    w_out_copy.start()

    def store_gate(piece, rows):
        gate[:, pl.ds(piece * 2 * head_dim, 2 * head_dim)] = rows

    project(0, store_gate)

    row = lax.broadcasted_iota(jnp.int32, bias.shape, 0)
    column = lax.broadcasted_iota(jnp.int32, bias.shape, 1)
    gap = (n_seq - 1) * tok + row - column
    slope = slope_ref[mine]
    logs = jnp.log(1.0 + jnp.maximum(gap, 0).astype(jnp.float32))
    bias[...] = jnp.where(gap >= 0, (0.5 * slope) * logs, OFF)

    @pl.when(side == 0)
    def _():
        mix_low[...] = jnp.zeros_like(mix_low)

    beams = beam_ref[...]
    subtree = beams >> 6
    found = jnp.zeros_like(beams)
    for index in range(map_ref.shape[0]):
        found = jnp.where(subtree == index, map_ref[index], found)
    stored = found * SUBT + (beams & (SUBT - 1))
    per_user = beams.shape[1]
    stored_row = jnp.concatenate([stored[u : u + 1] for u in range(USERS)], axis=1)
    node = lax.broadcasted_iota(jnp.int32, onehot.shape, 0)
    onehot[...] = jnp.where(node == stored_row, 1.0, 0.0).astype(jnp.bfloat16)

    starts = [0, blocks_ref[0, 0], blocks_ref[0, 0] + blocks_ref[0, 1]]
    lengths = [(blocks_ref[0, u] - 1) * BLK + tail_ref[0, u] for u in range(USERS)]

    def landed(ref, sem):
        pltpu.make_async_copy(ref, ref, sem).wait()

    def attend(block, first_key, low, high, bias_at):
        first = jnp.where(block >= starts[1], starts[1], 0)
        length = jnp.where(block >= starts[1], lengths[1], lengths[0])
        first = jnp.where(block >= starts[2], starts[2], first)
        length = jnp.where(block >= starts[2], lengths[2], length)
        queries = query[block]
        total = jnp.zeros((tok, head_dim), jnp.float32)
        for at in range(low, high, 2):
            end = min(at + 2, high)
            wide = (end - at) * tok
            keys = kv[0, at:end].reshape(wide, head_dim)
            values = kv[1, at:end].reshape(wide, head_dim)
            key_block = lax.broadcasted_iota(jnp.int32, (1, wide), 1) // tok + (first_key + at)
            seen = jnp.where(key_block >= first, 0.0, OFF)
            scores = lax.dot_general(
                queries, keys, (((1,), (1,)), ((), ())), preferred_element_type=jnp.float32
            )
            begin = bias_at + (at - low) * tok
            halves = scores + (bias[:, begin : begin + wide] + seen)
            weights = silu_of_half(halves).astype(jnp.bfloat16)
            total += jnp.dot(weights, values, preferred_element_type=jnp.float32)
        row = lax.broadcasted_iota(jnp.int32, (tok, head_dim), 0)
        live = (block - first) * tok + row < length
        return jnp.where(live, total, 0.0).astype(jnp.bfloat16)

    for place in range(heads):
        block = base + place
        landed(query.at[block], q_recv.at[block])
        for which in range(2):
            landed(kv.at[which, place], kv_recv.at[which, place])
        count = place + 1
        result[place] = attend(block, base, 0, count, (n_seq - count) * tok)

        @pl.when(mine != place)
        def _():
            remote(
                result.at[place], mix.at[mine], r_send.at[place], r_recv.at[mine], {"seq": block}
            ).start()

        @pl.when(mine == place)
        def _():
            pltpu.make_async_copy(result.at[place], mix.at[mine], r_recv.at[mine]).start()

    for step in range(1, n_dp):
        source = (dp + step) % n_dp
        came = table_buf.at[source, pl.ds(core * part_nodes, part_nodes)]
        landed(came, table_recv.at[source])
        copy = remote(came, came, table_fwd.at[step], table_relay.at[source], {"seq": sibling})
        copy.start()
        waits.append(copy)

    @pl.when(side == 0)
    def _():
        copies = []
        for step in range(heads):
            block = heads + step
            landed(query.at[block], q_recv.at[block])
            low = max(0, block + 1 - window)
            result[block] = attend(block, 0, low, heads, (n_seq - 1 - block + low) * tok)
            copy = remote(
                result.at[heads + step],
                mix_low.at[mine],
                r_send.at[heads + step],
                r_low_recv.at[mine],
                {"seq": block},
            )
            copy.start()
            copies.append(copy)
        for copy in copies:
            copy.wait_send()

    w_out_copy.wait()
    for source in range(heads):
        landed(mix.at[source], r_recv.at[source])

    @pl.when(side == 1)
    def _():
        for source in range(heads):
            landed(mix_low.at[source], r_low_recv.at[source])

    mixed = jnp.concatenate(
        [
            mix[head].astype(jnp.float32) + mix_low[head].astype(jnp.float32)
            for head in range(heads)
        ],
        axis=1,
    )
    gated = layer_norm(mixed) * out_gain_ref[...] * gate[...].astype(jnp.float32)
    out = jnp.dot(
        gated.astype(jnp.bfloat16), w_out_buf[...], preferred_element_type=jnp.float32
    )
    layer_rows = (x_ref[0].astype(jnp.float32) + out).astype(jnp.bfloat16)

    rows = 16
    which_user = lax.broadcasted_iota(jnp.int32, (rows, tok), 0)
    slot = lax.broadcasted_iota(jnp.int32, (rows, tok), 1) + me * tok
    last = jnp.full((rows, tok), -1, jnp.int32)
    for u in range(USERS):
        last = jnp.where(which_user == u, starts[u] * BLK + lengths[u] - 1, last)
    picker = jnp.where(slot == last, 1.0, 0.0).astype(jnp.bfloat16)
    states = jnp.dot(picker, layer_rows, preferred_element_type=jnp.float32).astype(jnp.bfloat16)
    pltpu.make_async_copy(table_ref, table_buf.at[dp], table_sem).wait()
    for step in range(1, n_dp):
        source = (dp + step) % n_dp
        came = table_buf.at[source, pl.ds((1 - core) * part_nodes, part_nodes)]
        pltpu.make_async_copy(came, came, table_relay.at[source]).wait()
    node_scores = lax.dot_general(
        states,
        table_buf[...].reshape(n_dp * nodes, width),
        (((1,), (1,)), ((), ())),
        preferred_element_type=jnp.float32,
    )
    pieces = [
        node_scores[u : u + 1, c * LANES : (c + 1) * LANES]
        for u in range(USERS)
        for c in range(chunks)
    ]
    spare = part_sent.shape[0] - len(pieces)
    if spare:
        pieces.append(jnp.zeros((spare, LANES), jnp.float32))
    part = jnp.concatenate(pieces, axis=0).astype(jnp.bfloat16)
    part_sent[...] = part
    part_recv[me] = part
    for step in far_first(n_seq):
        copy = remote(
            part_sent,
            part_recv.at[me],
            p_send.at[step],
            p_recv.at[me],
            {"seq": (me + step) % n_seq},
        )
        copy.start()
        waits.append(copy)

    layer_ref[0] = layer_rows

    for copy in waits:
        copy.wait_send()
    @pl.when(side == 1)
    def _():
        for step in range(heads):
            head = (mine + step) % heads
            remote(
                sent.at[0, head], query.at[me], cross_send.at[step], q_recv.at[me], {"seq": head}
            ).wait_send()

    for place in range(heads):

        @pl.when(mine != place)
        def _():
            remote(
                result.at[place],
                mix.at[mine],
                r_send.at[place],
                r_recv.at[mine],
                {"seq": base + place},
            ).wait_send()

    for step in far_first(n_seq):
        source = (me + step) % n_seq
        pltpu.make_async_copy(
            part_recv.at[source], part_recv.at[source], p_recv.at[source]
        ).wait()
    total = jnp.sum(part_recv[...].astype(jnp.float32), axis=0)
    users = [
        jnp.concatenate(
            [total[u * chunks + c : u * chunks + c + 1] for c in range(chunks)], axis=1
        )
        for u in range(USERS)
    ]
    users.append(jnp.zeros((rows - USERS, n_dp * nodes), jnp.float32))
    score_rows = jnp.concatenate(users, axis=0).astype(jnp.bfloat16)
    picked = jnp.dot(score_rows, onehot[...], preferred_element_type=jnp.float32)
    for u in range(USERS):
        scores_ref[u : u + 1] = picked[u : u + 1, u * per_user : (u + 1) * per_user]


def hand_over(layer_in, scores_in, layer_out, scores_out, layer_sem, scores_sem):
    layer = pltpu.make_async_copy(layer_in, layer_out, layer_sem)
    scores = pltpu.make_async_copy(scores_in, scores_out, scores_sem)
    layer.start()
    scores.start()
    layer.wait()
    scores.wait()


def body(
    n_dp,
    n_seq,
    tokens,
    in_gain,
    w_proj,
    out_gain,
    w_out,
    rab_slope,
    hist_blocks,
    hist_tail,
    node_table,
    subtree_map,
    beam_nodes,
):
    _, tok, width = tokens.shape
    heads = rab_slope.shape[0]
    head_dim = width // heads
    nodes = node_table.shape[0]
    assert n_seq == 2 * heads and tok == BLK
    part_rows = -(-USERS * n_dp * nodes // LANES // 16) * 16
    vmem = pl.BlockSpec(memory_space=pltpu.VMEM)
    smem = pl.BlockSpec(memory_space=pltpu.SMEM)
    hbm = pl.BlockSpec(memory_space=pl.ANY)
    dma = pltpu.SemaphoreType.DMA
    bf16 = jnp.bfloat16
    layer_out, scores = pl.pallas_call(
        functools.partial(layer_kernel, n_dp, n_seq),
        out_shape=(
            jax.ShapeDtypeStruct(tokens.shape, bf16),
            jax.ShapeDtypeStruct(beam_nodes.shape, jnp.float32),
        ),
        in_specs=[hbm, vmem, hbm, vmem, hbm, smem, smem, smem, hbm, smem, vmem],
        out_specs=(vmem, vmem),
        scratch_shapes=[
            pltpu.VMEM(tokens.shape, bf16),
            pltpu.VMEM((4, width, width), bf16),
            pltpu.VMEM((width, width), bf16),
            pltpu.VMEM((n_dp, nodes, width), bf16),
            pltpu.VMEM((3, heads, tok, head_dim), bf16),
            pltpu.VMEM((tok, width), bf16),
            pltpu.VMEM((2, heads, tok, head_dim), bf16),
            pltpu.VMEM((n_seq, tok, head_dim), bf16),
            pltpu.VMEM((n_seq, tok, head_dim), bf16),
            pltpu.VMEM((heads, tok, head_dim), bf16),
            pltpu.VMEM((heads, tok, head_dim), bf16),
            pltpu.VMEM((tok, n_seq * tok), jnp.float32),
            pltpu.VMEM((part_rows, LANES), bf16),
            pltpu.VMEM((n_seq, part_rows, LANES), bf16),
            pltpu.VMEM((n_dp * nodes, USERS * beam_nodes.shape[1]), bf16),
            dma,
            dma((4,)),
            dma,
            dma,
            dma((n_dp,)),
            dma((n_dp,)),
            dma((n_dp,)),
            dma((n_dp,)),
            dma((2, heads)),
            dma((2, heads)),
            dma((heads,)),
            dma((heads,)),
            dma((n_seq,)),
            dma((n_seq,)),
            dma((heads,)),
            dma((heads,)),
            dma((n_seq,)),
            dma((n_seq,)),
        ],
        compiler_params=pltpu.CompilerParams(
            collective_id=0, has_side_effects=True, vmem_limit_bytes=56 * 1024 * 1024
        ),
    )(
        tokens,
        in_gain.reshape(1, width),
        w_proj,
        out_gain.reshape(1, width),
        w_out,
        rab_slope,
        hist_blocks,
        hist_tail,
        node_table,
        subtree_map,
        beam_nodes,
    )
    return pl.pallas_call(
        hand_over,
        out_shape=(
            jax.ShapeDtypeStruct(layer_out.shape, bf16),
            jax.ShapeDtypeStruct(scores.shape, jnp.float32),
        ),
        in_specs=[vmem, vmem],
        out_specs=(hbm, hbm),
        scratch_shapes=[dma, dma],
    )(layer_out, scores)


def solution(mesh):
    placed = (
        P("dp", "seq", None),
        P(),
        P(),
        P(),
        P(),
        P(),
        P("dp", None),
        P("dp", None),
        P("dp", None),
        P(),
        P("dp", "seq"),
    )
    return jax.shard_map(
        functools.partial(body, mesh.shape["dp"], mesh.shape["seq"]),
        mesh=mesh,
        in_specs=placed,
        out_specs=(P("dp", "seq", None), P("dp", "seq")),
        check_vma=False,
    )
```

```python
import functools

import jax
import jax.numpy as jnp
from jax import lax
from jax.experimental import pallas as pl
from jax.experimental.pallas import tpu as pltpu
from jax.sharding import PartitionSpec as P

BLK = 128
SUBT = 64
USERS = 3
LANES = 128
MESH = pl.DeviceIdType.MESH
OFF = -1e30


def layer_norm(rows):
    centred = rows - jnp.mean(rows, axis=-1, keepdims=True)
    spread = jnp.mean(centred * centred, axis=-1, keepdims=True)
    return centred * lax.rsqrt(spread + 1e-05)


def silu_of_half(half):
    return half + half * jnp.tanh(half)


def far_first(count):
    order = []
    for step in range(count // 2):
        for offset in (count // 2 - step, count // 2 + step):
            if 0 < offset < count and offset not in order:
                order.append(offset)
    return order


def layer_kernel(
    n_dp,
    n_seq,
    x_hbm,
    in_gain_ref,
    w_proj_ref,
    out_gain_ref,
    w_out_ref,
    slope_ref,
    blocks_ref,
    tail_ref,
    table_ref,
    map_ref,
    beam_ref,
    layer_ref,
    scores_ref,
    x_ref,
    w_buf,
    w_out_buf,
    table_buf,
    sent,
    gate,
    held,
    upper,
    result,
    mix,
    mix_low,
    bias,
    part_sent,
    part_recv,
    onehot,
    x_sem,
    w_sem,
    w_out_sem,
    table_sem,
    table_send,
    table_recv,
    table_fwd,
    table_relay,
    h_send,
    h_recv,
    cross_send,
    u_recv,
    r_send,
    r_recv,
    r_low_recv,
    p_send,
    p_recv,
):
    tok, width = x_ref.shape[1:]
    heads, _, head_dim = mix.shape
    nodes = table_ref.shape[0]
    chunks = n_dp * nodes // LANES
    me = lax.axis_index("seq")
    dp = lax.axis_index("dp")
    side, mine = me // heads, me % heads
    base = side * heads
    window = heads + 2
    core = me % 2
    sibling = me + 1 - 2 * core

    def remote(src, dst, send_sem, recv_sem, where):
        return pltpu.make_async_remote_copy(
            src_ref=src,
            dst_ref=dst,
            send_sem=send_sem,
            recv_sem=recv_sem,
            device_id=where,
            device_id_type=MESH,
        )

    x_copy = pltpu.make_async_copy(x_hbm, x_ref, x_sem)
    x_copy.start()
    order = (1, 2, 3, 0)
    w_copies = {
        part: pltpu.make_async_copy(
            w_proj_ref.at[:, pl.ds(part * width, width)], w_buf.at[part], w_sem.at[part]
        )
        for part in order
    }
    for part in order:
        w_copies[part].start()

    pltpu.make_async_copy(table_ref, table_buf.at[dp], table_sem).start()
    barrier = pltpu.get_barrier_semaphore()
    for step in range(1, n_seq):
        pl.semaphore_signal(
            barrier, inc=1, device_id={"seq": (me + step) % n_seq}, device_id_type=MESH
        )
    for step in range(1, n_dp):
        pl.semaphore_signal(
            barrier, inc=1, device_id={"dp": (dp + step) % n_dp}, device_id_type=MESH
        )

    x_copy.wait()
    x_rows = x_ref[0].astype(jnp.float32)
    normed = (layer_norm(x_rows) * in_gain_ref[...]).astype(jnp.bfloat16)

    def project(part, store):
        w_copies[part].wait()
        for piece in range(heads // 2):
            columns = pl.ds(piece * 2 * head_dim, 2 * head_dim)
            out = jnp.dot(normed, w_buf[part, :, columns], preferred_element_type=jnp.float32)
            rows = silu_of_half(0.5 * out)
            if part == 1:
                rows = rows * (0.5 * head_dim ** (-0.5))
            store(piece, rows.astype(jnp.bfloat16))

    def store_heads(slot):
        def store(piece, rows):
            sent[2 * piece, slot] = rows[:, :head_dim]
            sent[2 * piece + 1, slot] = rows[:, head_dim:]

        return store

    waits = []
    project(1, store_heads(0))
    pl.semaphore_wait(barrier, n_seq - 1 + n_dp - 1)

    @pl.when(side == 1)
    def _():
        for step in range(heads):
            head = (mine + step) % heads
            remote(
                sent.at[head, 0], upper.at[mine], cross_send.at[step], u_recv.at[mine], {"seq": head}
            ).start()

    project(2, store_heads(1))
    project(3, store_heads(2))
    for step in range(heads):
        head = (mine + step) % heads
        if step == 0:
            pltpu.make_async_copy(sent.at[head], held.at[mine], h_recv.at[mine]).start()
        else:
            copy = remote(
                sent.at[head],
                held.at[mine],
                h_send.at[step],
                h_recv.at[mine],
                {"seq": base + head},
            )
            copy.start()
            waits.append(copy)

    part_nodes = nodes // 2
    pltpu.make_async_copy(table_ref, table_buf.at[dp], table_sem).wait()
    for step in range(1, n_dp):
        own_rows = pl.ds(core * part_nodes, part_nodes)
        copy = remote(
            table_buf.at[dp, own_rows],
            table_buf.at[dp, own_rows],
            table_send.at[step],
            table_recv.at[dp],
            {"dp": (dp + step) % n_dp},
        )
        copy.start()
        waits.append(copy)
    w_out_copy = pltpu.make_async_copy(w_out_ref, w_out_buf, w_out_sem)
    w_out_copy.start()

    def store_gate(piece, rows):
        gate[:, pl.ds(piece * 2 * head_dim, 2 * head_dim)] = rows

    project(0, store_gate)

    row = lax.broadcasted_iota(jnp.int32, bias.shape, 0)
    column = lax.broadcasted_iota(jnp.int32, bias.shape, 1)
    gap = (n_seq - 1) * tok + row - column
    slope = slope_ref[mine]
    logs = jnp.log(1.0 + jnp.maximum(gap, 0).astype(jnp.float32))
    bias[...] = jnp.where(gap >= 0, (0.5 * slope) * logs, OFF)

    @pl.when(side == 0)
    def _():
        mix_low[...] = jnp.zeros_like(mix_low)

    beams = beam_ref[...]
    subtree = beams >> 6
    found = jnp.zeros_like(beams)
    for index in range(map_ref.shape[0]):
        found = jnp.where(subtree == index, map_ref[index], found)
    stored = found * SUBT + (beams & (SUBT - 1))
    per_user = beams.shape[1]
    stored_row = jnp.concatenate([stored[u : u + 1] for u in range(USERS)], axis=1)
    node = lax.broadcasted_iota(jnp.int32, onehot.shape, 0)
    onehot[...] = jnp.where(node == stored_row, 1.0, 0.0).astype(jnp.bfloat16)

    starts = [0, blocks_ref[0, 0], blocks_ref[0, 0] + blocks_ref[0, 1]]
    lengths = [(blocks_ref[0, u] - 1) * BLK + tail_ref[0, u] for u in range(USERS)]

    def landed(ref, sem):
        pltpu.make_async_copy(ref, ref, sem).wait()

    def attend(block, queries, first_key, low, high, bias_at):
        first = jnp.where(block >= starts[1], starts[1], 0)
        length = jnp.where(block >= starts[1], lengths[1], lengths[0])
        first = jnp.where(block >= starts[2], starts[2], first)
        length = jnp.where(block >= starts[2], lengths[2], length)
        total = jnp.zeros((tok, head_dim), jnp.float32)
        for at in range(low, high, 2):
            end = min(at + 2, high)
            wide = (end - at) * tok
            keys = held[at:end, 1].reshape(wide, head_dim)
            values = held[at:end, 2].reshape(wide, head_dim)
            key_block = lax.broadcasted_iota(jnp.int32, (1, wide), 1) // tok + (first_key + at)
            seen = jnp.where(key_block >= first, 0.0, OFF)
            scores = lax.dot_general(
                queries, keys, (((1,), (1,)), ((), ())), preferred_element_type=jnp.float32
            )
            begin = bias_at + (at - low) * tok
            halves = scores + (bias[:, begin : begin + wide] + seen)
            weights = silu_of_half(halves).astype(jnp.bfloat16)
            total += jnp.dot(weights, values, preferred_element_type=jnp.float32)
        row = lax.broadcasted_iota(jnp.int32, (tok, head_dim), 0)
        live = (block - first) * tok + row < length
        return jnp.where(live, total, 0.0).astype(jnp.bfloat16)

    for place in range(heads):
        block = base + place
        landed(held.at[place], h_recv.at[place])
        count = place + 1
        result[place] = attend(block, held[place, 0], base, 0, count, (n_seq - count) * tok)

        @pl.when(mine != place)
        def _():
            remote(
                result.at[place], mix.at[mine], r_send.at[place], r_recv.at[mine], {"seq": block}
            ).start()

        @pl.when(mine == place)
        def _():
            pltpu.make_async_copy(result.at[place], mix.at[mine], r_recv.at[mine]).start()

    for step in range(1, n_dp):
        source = (dp + step) % n_dp
        came = table_buf.at[source, pl.ds(core * part_nodes, part_nodes)]
        landed(came, table_recv.at[source])
        copy = remote(came, came, table_fwd.at[step], table_relay.at[source], {"seq": sibling})
        copy.start()
        waits.append(copy)

    @pl.when(side == 0)
    def _():
        copies = []
        for step in range(heads):
            block = heads + step
            landed(upper.at[step], u_recv.at[step])
            low = max(0, block + 1 - window)
            result[block] = attend(
                block, upper[step], 0, low, heads, (n_seq - 1 - block + low) * tok
            )
            copy = remote(
                result.at[heads + step],
                mix_low.at[mine],
                r_send.at[heads + step],
                r_low_recv.at[mine],
                {"seq": block},
            )
            copy.start()
            copies.append(copy)
        for copy in copies:
            copy.wait_send()

    w_out_copy.wait()
    for source in range(heads):
        landed(mix.at[source], r_recv.at[source])

    @pl.when(side == 1)
    def _():
        for source in range(heads):
            landed(mix_low.at[source], r_low_recv.at[source])

    mixed = jnp.concatenate(
        [
            mix[head].astype(jnp.float32) + mix_low[head].astype(jnp.float32)
            for head in range(heads)
        ],
        axis=1,
    )
    gated = layer_norm(mixed) * out_gain_ref[...] * gate[...].astype(jnp.float32)
    out = jnp.dot(
        gated.astype(jnp.bfloat16), w_out_buf[...], preferred_element_type=jnp.float32
    )
    layer_rows = (x_ref[0].astype(jnp.float32) + out).astype(jnp.bfloat16)

    rows = 16
    which_user = lax.broadcasted_iota(jnp.int32, (rows, tok), 0)
    slot = lax.broadcasted_iota(jnp.int32, (rows, tok), 1) + me * tok
    last = jnp.full((rows, tok), -1, jnp.int32)
    for u in range(USERS):
        last = jnp.where(which_user == u, starts[u] * BLK + lengths[u] - 1, last)
    picker = jnp.where(slot == last, 1.0, 0.0).astype(jnp.bfloat16)
    states = jnp.dot(picker, layer_rows, preferred_element_type=jnp.float32).astype(jnp.bfloat16)
    for step in range(1, n_dp):
        source = (dp + step) % n_dp
        came = table_buf.at[source, pl.ds((1 - core) * part_nodes, part_nodes)]
        pltpu.make_async_copy(came, came, table_relay.at[source]).wait()
    node_scores = lax.dot_general(
        states,
        table_buf[...].reshape(n_dp * nodes, width),
        (((1,), (1,)), ((), ())),
        preferred_element_type=jnp.float32,
    )
    pieces = [
        node_scores[u : u + 1, c * LANES : (c + 1) * LANES]
        for u in range(USERS)
        for c in range(chunks)
    ]
    spare = part_sent.shape[0] - len(pieces)
    if spare:
        pieces.append(jnp.zeros((spare, LANES), jnp.float32))
    part = jnp.concatenate(pieces, axis=0).astype(jnp.bfloat16)
    part_sent[...] = part
    part_recv[me] = part
    for step in far_first(n_seq):
        copy = remote(
            part_sent,
            part_recv.at[me],
            p_send.at[step],
            p_recv.at[me],
            {"seq": (me + step) % n_seq},
        )
        copy.start()
        waits.append(copy)

    layer_ref[0] = layer_rows

    for copy in waits:
        copy.wait_send()
    @pl.when(side == 1)
    def _():
        for step in range(heads):
            head = (mine + step) % heads
            remote(
                sent.at[head, 0], upper.at[mine], cross_send.at[step], u_recv.at[mine], {"seq": head}
            ).wait_send()

    for place in range(heads):

        @pl.when(mine != place)
        def _():
            remote(
                result.at[place],
                mix.at[mine],
                r_send.at[place],
                r_recv.at[mine],
                {"seq": base + place},
            ).wait_send()

    for step in far_first(n_seq):
        source = (me + step) % n_seq
        pltpu.make_async_copy(
            part_recv.at[source], part_recv.at[source], p_recv.at[source]
        ).wait()
    total = jnp.sum(part_recv[...].astype(jnp.float32), axis=0)
    users = [
        jnp.concatenate(
            [total[u * chunks + c : u * chunks + c + 1] for c in range(chunks)], axis=1
        )
        for u in range(USERS)
    ]
    users.append(jnp.zeros((rows - USERS, n_dp * nodes), jnp.float32))
    score_rows = jnp.concatenate(users, axis=0).astype(jnp.bfloat16)
    picked = jnp.dot(score_rows, onehot[...], preferred_element_type=jnp.float32)
    for u in range(USERS):
        scores_ref[u : u + 1] = picked[u : u + 1, u * per_user : (u + 1) * per_user]


def hand_over(layer_in, scores_in, layer_out, scores_out, layer_sem, scores_sem):
    layer = pltpu.make_async_copy(layer_in, layer_out, layer_sem)
    scores = pltpu.make_async_copy(scores_in, scores_out, scores_sem)
    layer.start()
    scores.start()
    layer.wait()
    scores.wait()


def body(
    n_dp,
    n_seq,
    tokens,
    in_gain,
    w_proj,
    out_gain,
    w_out,
    rab_slope,
    hist_blocks,
    hist_tail,
    node_table,
    subtree_map,
    beam_nodes,
):
    _, tok, width = tokens.shape
    heads = rab_slope.shape[0]
    head_dim = width // heads
    nodes = node_table.shape[0]
    assert n_seq == 2 * heads and tok == BLK
    part_rows = -(-USERS * n_dp * nodes // LANES // 16) * 16
    vmem = pl.BlockSpec(memory_space=pltpu.VMEM)
    smem = pl.BlockSpec(memory_space=pltpu.SMEM)
    hbm = pl.BlockSpec(memory_space=pl.ANY)
    dma = pltpu.SemaphoreType.DMA
    bf16 = jnp.bfloat16
    layer_out, scores = pl.pallas_call(
        functools.partial(layer_kernel, n_dp, n_seq),
        out_shape=(
            jax.ShapeDtypeStruct(tokens.shape, bf16),
            jax.ShapeDtypeStruct(beam_nodes.shape, jnp.float32),
        ),
        in_specs=[hbm, vmem, hbm, vmem, hbm, smem, smem, smem, hbm, smem, vmem],
        out_specs=(vmem, vmem),
        scratch_shapes=[
            pltpu.VMEM(tokens.shape, bf16),
            pltpu.VMEM((4, width, width), bf16),
            pltpu.VMEM((width, width), bf16),
            pltpu.VMEM((n_dp, nodes, width), bf16),
            pltpu.VMEM((heads, 3, tok, head_dim), bf16),
            pltpu.VMEM((tok, width), bf16),
            pltpu.VMEM((heads, 3, tok, head_dim), bf16),
            pltpu.VMEM((heads, tok, head_dim), bf16),
            pltpu.VMEM((n_seq, tok, head_dim), bf16),
            pltpu.VMEM((heads, tok, head_dim), bf16),
            pltpu.VMEM((heads, tok, head_dim), bf16),
            pltpu.VMEM((tok, n_seq * tok), jnp.float32),
            pltpu.VMEM((part_rows, LANES), bf16),
            pltpu.VMEM((n_seq, part_rows, LANES), bf16),
            pltpu.VMEM((n_dp * nodes, USERS * beam_nodes.shape[1]), bf16),
            dma,
            dma((4,)),
            dma,
            dma,
            dma((n_dp,)),
            dma((n_dp,)),
            dma((n_dp,)),
            dma((n_dp,)),
            dma((heads,)),
            dma((heads,)),
            dma((heads,)),
            dma((heads,)),
            dma((n_seq,)),
            dma((heads,)),
            dma((heads,)),
            dma((n_seq,)),
            dma((n_seq,)),
        ],
        compiler_params=pltpu.CompilerParams(
            collective_id=0, has_side_effects=True, vmem_limit_bytes=56 * 1024 * 1024
        ),
    )(
        tokens,
        in_gain.reshape(1, width),
        w_proj,
        out_gain.reshape(1, width),
        w_out,
        rab_slope,
        hist_blocks,
        hist_tail,
        node_table,
        subtree_map,
        beam_nodes,
    )
    return pl.pallas_call(
        hand_over,
        out_shape=(
            jax.ShapeDtypeStruct(layer_out.shape, bf16),
            jax.ShapeDtypeStruct(scores.shape, jnp.float32),
        ),
        in_specs=[vmem, vmem],
        out_specs=(hbm, hbm),
        scratch_shapes=[dma, dma],
    )(layer_out, scores)


def solution(mesh):
    placed = (
        P("dp", "seq", None),
        P(),
        P(),
        P(),
        P(),
        P(),
        P("dp", None),
        P("dp", None),
        P("dp", None),
        P(),
        P("dp", "seq"),
    )
    return jax.shard_map(
        functools.partial(body, mesh.shape["dp"], mesh.shape["seq"]),
        mesh=mesh,
        in_specs=placed,
        out_specs=(P("dp", "seq", None), P("dp", "seq")),
        check_vma=False,
    )
```

```python
import functools

import jax
import jax.numpy as jnp
from jax import lax
from jax.experimental import pallas as pl
from jax.experimental.pallas import tpu as pltpu
from jax.sharding import PartitionSpec as P

BLK = 128
SUBT = 64
USERS = 3
LANES = 128
MESH = pl.DeviceIdType.MESH
OFF = -1e30


def layer_norm(rows):
    centred = rows - jnp.mean(rows, axis=-1, keepdims=True)
    spread = jnp.mean(centred * centred, axis=-1, keepdims=True)
    return centred * lax.rsqrt(spread + 1e-05)


def silu_of_half(half):
    return half + half * jnp.tanh(half)


def far_first(count):
    order = []
    for step in range(count // 2):
        for offset in (count // 2 - step, count // 2 + step):
            if 0 < offset < count and offset not in order:
                order.append(offset)
    return order


def layer_kernel(
    n_dp,
    n_seq,
    x_hbm,
    in_gain_ref,
    w_proj_ref,
    out_gain_ref,
    w_out_ref,
    slope_ref,
    blocks_ref,
    tail_ref,
    table_ref,
    map_ref,
    beam_ref,
    layer_ref,
    scores_ref,
    x_ref,
    w_buf,
    w_out_buf,
    table_buf,
    sent,
    normed_ref,
    held,
    upper,
    result,
    mix,
    mix_low,
    bias,
    part_sent,
    part_recv,
    onehot,
    x_sem,
    w_sem,
    w_out_sem,
    table_sem,
    table_send,
    table_recv,
    table_fwd,
    table_relay,
    h_send,
    h_recv,
    cross_send,
    u_recv,
    r_send,
    r_recv,
    r_low_recv,
    p_send,
    p_recv,
):
    tok, width = x_ref.shape[1:]
    heads, _, head_dim = mix.shape
    nodes = table_ref.shape[0]
    chunks = n_dp * nodes // LANES
    me = lax.axis_index("seq")
    dp = lax.axis_index("dp")
    side, mine = me // heads, me % heads
    base = side * heads
    window = heads + 2
    core = me % 2
    sibling = me + 1 - 2 * core

    def remote(src, dst, send_sem, recv_sem, where):
        return pltpu.make_async_remote_copy(
            src_ref=src,
            dst_ref=dst,
            send_sem=send_sem,
            recv_sem=recv_sem,
            device_id=where,
            device_id_type=MESH,
        )

    x_copy = pltpu.make_async_copy(x_hbm, x_ref, x_sem)
    x_copy.start()
    order = (1, 2, 3, 0)
    w_copies = {
        part: pltpu.make_async_copy(
            w_proj_ref.at[:, pl.ds(part * width, width)], w_buf.at[part], w_sem.at[part]
        )
        for part in order
    }
    for part in order:
        w_copies[part].start()

    pltpu.make_async_copy(table_ref, table_buf.at[dp], table_sem).start()
    barrier = pltpu.get_barrier_semaphore()
    for step in range(1, n_seq):
        pl.semaphore_signal(
            barrier, inc=1, device_id={"seq": (me + step) % n_seq}, device_id_type=MESH
        )
    for step in range(1, n_dp):
        pl.semaphore_signal(
            barrier, inc=1, device_id={"dp": (dp + step) % n_dp}, device_id_type=MESH
        )

    x_copy.wait()
    x_rows = x_ref[0].astype(jnp.float32)
    normed = (layer_norm(x_rows) * in_gain_ref[...]).astype(jnp.bfloat16)

    pieces = heads // 2
    pair = 2 * head_dim
    normed_ref[...] = normed

    def project(step, carry):
        slot, piece = step // pieces, step % pieces
        part = (slot + 1) % 4

        @pl.when(piece == 0)
        def _():
            pltpu.make_async_copy(
                w_proj_ref.at[:, pl.ds(0, width)], w_buf.at[part], w_sem.at[part]
            ).wait()

        columns = pl.ds(pl.multiple_of(piece * pair, pair), pair)
        out = jnp.dot(normed_ref[...], w_buf[part, :, columns], preferred_element_type=jnp.float32)
        scale = jnp.where(part == 1, 0.5 * head_dim ** (-0.5), 1.0)
        rows = (silu_of_half(0.5 * out) * scale).astype(jnp.bfloat16)
        sent[2 * piece, slot] = rows[:, :head_dim]
        sent[2 * piece + 1, slot] = rows[:, head_dim:]
        return carry

    waits = []
    lax.fori_loop(0, pieces, project, 0)
    pl.semaphore_wait(barrier, n_seq - 1 + n_dp - 1)

    @pl.when(side == 1)
    def _():
        for step in range(heads):
            head = (mine + step) % heads
            remote(
                sent.at[head, 0], upper.at[mine], cross_send.at[step], u_recv.at[mine], {"seq": head}
            ).start()

    lax.fori_loop(pieces, 3 * pieces, project, 0)
    for step in range(heads):
        head = (mine + step) % heads
        if step == 0:
            pltpu.make_async_copy(sent.at[head, 0:3], held.at[mine], h_recv.at[mine]).start()
        else:
            copy = remote(
                sent.at[head, 0:3],
                held.at[mine],
                h_send.at[step],
                h_recv.at[mine],
                {"seq": base + head},
            )
            copy.start()
            waits.append(copy)

    part_nodes = nodes // 2
    pltpu.make_async_copy(table_ref, table_buf.at[dp], table_sem).wait()
    for step in range(1, n_dp):
        own_rows = pl.ds(core * part_nodes, part_nodes)
        copy = remote(
            table_buf.at[dp, own_rows],
            table_buf.at[dp, own_rows],
            table_send.at[step],
            table_recv.at[dp],
            {"dp": (dp + step) % n_dp},
        )
        copy.start()
        waits.append(copy)
    w_out_copy = pltpu.make_async_copy(w_out_ref, w_out_buf, w_out_sem)
    w_out_copy.start()

    lax.fori_loop(3 * pieces, 4 * pieces, project, 0)

    slope = slope_ref[mine]

    def place_bias(delta, carry):
        row = lax.broadcasted_iota(jnp.int32, bias.shape[1:], 0)
        column = lax.broadcasted_iota(jnp.int32, bias.shape[1:], 1)
        gap = delta * 2 * tok + row - column
        logs = jnp.log(1.0 + jnp.maximum(gap, 0).astype(jnp.float32))
        bias[delta] = jnp.where(gap >= 0, (0.5 * slope) * logs, OFF)
        return carry

    lax.fori_loop(0, bias.shape[0], place_bias, 0)

    @pl.when(side == 0)
    def _():
        mix_low[...] = jnp.zeros_like(mix_low)

    beams = beam_ref[...]
    subtree = beams >> 6
    found = jnp.zeros_like(beams)
    for index in range(map_ref.shape[0]):
        found = jnp.where(subtree == index, map_ref[index], found)
    stored = found * SUBT + (beams & (SUBT - 1))
    per_user = beams.shape[1]
    stored_row = jnp.concatenate([stored[u : u + 1] for u in range(USERS)], axis=1)
    node = lax.broadcasted_iota(jnp.int32, onehot.shape, 0)
    onehot[...] = jnp.where(node == stored_row, 1.0, 0.0).astype(jnp.bfloat16)

    starts = [0, blocks_ref[0, 0], blocks_ref[0, 0] + blocks_ref[0, 1]]
    lengths = [(blocks_ref[0, u] - 1) * BLK + tail_ref[0, u] for u in range(USERS)]

    def landed(ref, sem):
        pltpu.make_async_copy(ref, ref, sem).wait()

    def user_of(block):
        first = jnp.where(block >= starts[1], starts[1], 0)
        length = jnp.where(block >= starts[1], lengths[1], lengths[0])
        first = jnp.where(block >= starts[2], starts[2], first)
        length = jnp.where(block >= starts[2], lengths[2], length)
        return first, length

    def attend(block, queries, first_key, low, high):
        row = lax.broadcasted_iota(jnp.int32, (2 * tok, 1), 0)
        (first, length), (next_first, next_length) = user_of(block), user_of(block + 1)
        first_row = jnp.where(row < tok, first, next_first)
        end_row = jnp.where(row < tok, first * tok + length, next_first * tok + next_length)
        column = lax.broadcasted_iota(jnp.int32, (1, 2 * tok), 1)

        def tile(at, total):
            keys = held[pl.ds(2 * at, 2), 1].reshape(2 * tok, head_dim)
            values = held[pl.ds(2 * at, 2), 2].reshape(2 * tok, head_dim)
            key_block = jnp.where(column < tok, 0, 1) + (first_key + 2 * at)
            scores = lax.dot_general(
                queries, keys, (((1,), (1,)), ((), ())), preferred_element_type=jnp.float32
            )
            halves = scores + bias[(block - first_key) // 2 - at]
            halves = jnp.where(key_block >= first_row, halves, OFF)
            weights = silu_of_half(halves).astype(jnp.bfloat16)
            return total + jnp.dot(weights, values, preferred_element_type=jnp.float32)

        total = lax.fori_loop(low, high, tile, jnp.zeros((2 * tok, head_dim), jnp.float32))
        live = block * tok + row < end_row
        rows = jnp.where(live, total, 0.0).astype(jnp.bfloat16)
        result[pl.ds(block - base, 2)] = rows.reshape(2, tok, head_dim)

    def own_half(at, carry):
        for place in (2 * at, 2 * at + 1):
            landed(held.at[place], h_recv.at[place])
        queries = held[pl.ds(2 * at, 2), 0].reshape(2 * tok, head_dim)
        attend(base + 2 * at, queries, base, 0, at + 1)
        for place in (2 * at, 2 * at + 1):

            @pl.when(mine != place)
            def _():
                remote(
                    result.at[place],
                    mix.at[mine],
                    r_send.at[place],
                    r_recv.at[mine],
                    {"seq": base + place},
                ).start()

            @pl.when(mine == place)
            def _():
                pltpu.make_async_copy(result.at[place], mix.at[mine], r_recv.at[mine]).start()

        return carry

    lax.fori_loop(0, heads // 2, own_half, 0)

    for step in range(1, n_dp):
        source = (dp + step) % n_dp
        came = table_buf.at[source, pl.ds(core * part_nodes, part_nodes)]
        landed(came, table_recv.at[source])
        copy = remote(came, came, table_fwd.at[step], table_relay.at[source], {"seq": sibling})
        copy.start()
        waits.append(copy)

    @pl.when(side == 0)
    def _():
        def low_half(at, carry):
            for step in (2 * at, 2 * at + 1):
                landed(upper.at[step], u_recv.at[step])
            queries = upper[pl.ds(2 * at, 2)].reshape(2 * tok, head_dim)
            low = jnp.maximum(at + heads // 2 - window // 2, 0)
            attend(heads + 2 * at, queries, 0, low, heads // 2)
            for block in (heads + 2 * at, heads + 2 * at + 1):
                remote(
                    result.at[block],
                    mix_low.at[mine],
                    r_send.at[block],
                    r_low_recv.at[mine],
                    {"seq": block},
                ).start()
            return carry

        lax.fori_loop(0, heads // 2, low_half, 0)
        for block in range(heads, n_seq):
            remote(
                result.at[block],
                mix_low.at[mine],
                r_send.at[block],
                r_low_recv.at[mine],
                {"seq": block},
            ).wait_send()

    w_out_copy.wait()
    for source in range(heads):
        landed(mix.at[source], r_recv.at[source])

    @pl.when(side == 1)
    def _():
        for source in range(heads):
            landed(mix_low.at[source], r_low_recv.at[source])

    mixed = jnp.concatenate(
        [
            mix[head].astype(jnp.float32) + mix_low[head].astype(jnp.float32)
            for head in range(heads)
        ],
        axis=1,
    )
    gate = jnp.concatenate([sent[head, 3] for head in range(heads)], axis=1)
    gated = layer_norm(mixed) * out_gain_ref[...] * gate.astype(jnp.float32)
    normed_ref[...] = gated.astype(jnp.bfloat16)

    def project_out(piece, carry):
        columns = pl.ds(pl.multiple_of(piece * pair, pair), pair)
        out = jnp.dot(normed_ref[...], w_out_buf[:, columns], preferred_element_type=jnp.float32)
        layer_ref[0, :, columns] = (x_ref[0, :, columns].astype(jnp.float32) + out).astype(
            jnp.bfloat16
        )
        return carry

    lax.fori_loop(0, pieces, project_out, 0)

    rows = 16
    which_user = lax.broadcasted_iota(jnp.int32, (rows, tok), 0)
    slot = lax.broadcasted_iota(jnp.int32, (rows, tok), 1) + me * tok
    last = jnp.full((rows, tok), -1, jnp.int32)
    for u in range(USERS):
        last = jnp.where(which_user == u, starts[u] * BLK + lengths[u] - 1, last)
    picker = jnp.where(slot == last, 1.0, 0.0).astype(jnp.bfloat16)
    states = jnp.dot(picker, layer_ref[0], preferred_element_type=jnp.float32).astype(jnp.bfloat16)
    for step in range(1, n_dp):
        source = (dp + step) % n_dp
        came = table_buf.at[source, pl.ds((1 - core) * part_nodes, part_nodes)]
        pltpu.make_async_copy(came, came, table_relay.at[source]).wait()
    node_scores = lax.dot_general(
        states,
        table_buf[...].reshape(n_dp * nodes, width),
        (((1,), (1,)), ((), ())),
        preferred_element_type=jnp.float32,
    )
    pieces = [
        node_scores[u : u + 1, c * LANES : (c + 1) * LANES]
        for u in range(USERS)
        for c in range(chunks)
    ]
    spare = part_sent.shape[0] - len(pieces)
    if spare:
        pieces.append(jnp.zeros((spare, LANES), jnp.float32))
    part = jnp.concatenate(pieces, axis=0).astype(jnp.bfloat16)
    part_sent[...] = part
    part_recv[me] = part
    for step in far_first(n_seq):
        copy = remote(
            part_sent,
            part_recv.at[me],
            p_send.at[step],
            p_recv.at[me],
            {"seq": (me + step) % n_seq},
        )
        copy.start()
        waits.append(copy)

    for copy in waits:
        copy.wait_send()
    @pl.when(side == 1)
    def _():
        for step in range(heads):
            head = (mine + step) % heads
            remote(
                sent.at[head, 0], upper.at[mine], cross_send.at[step], u_recv.at[mine], {"seq": head}
            ).wait_send()

    for place in range(heads):

        @pl.when(mine != place)
        def _():
            remote(
                result.at[place],
                mix.at[mine],
                r_send.at[place],
                r_recv.at[mine],
                {"seq": base + place},
            ).wait_send()

    for step in far_first(n_seq):
        source = (me + step) % n_seq
        pltpu.make_async_copy(
            part_recv.at[source], part_recv.at[source], p_recv.at[source]
        ).wait()
    total = jnp.sum(part_recv[...].astype(jnp.float32), axis=0)
    users = [
        jnp.concatenate(
            [total[u * chunks + c : u * chunks + c + 1] for c in range(chunks)], axis=1
        )
        for u in range(USERS)
    ]
    users.append(jnp.zeros((rows - USERS, n_dp * nodes), jnp.float32))
    score_rows = jnp.concatenate(users, axis=0).astype(jnp.bfloat16)
    picked = jnp.dot(score_rows, onehot[...], preferred_element_type=jnp.float32)
    for u in range(USERS):
        scores_ref[u : u + 1] = picked[u : u + 1, u * per_user : (u + 1) * per_user]


def hand_over(layer_in, scores_in, layer_out, scores_out, layer_sem, scores_sem):
    layer = pltpu.make_async_copy(layer_in, layer_out, layer_sem)
    scores = pltpu.make_async_copy(scores_in, scores_out, scores_sem)
    layer.start()
    scores.start()
    layer.wait()
    scores.wait()


def body(
    n_dp,
    n_seq,
    tokens,
    in_gain,
    w_proj,
    out_gain,
    w_out,
    rab_slope,
    hist_blocks,
    hist_tail,
    node_table,
    subtree_map,
    beam_nodes,
):
    _, tok, width = tokens.shape
    heads = rab_slope.shape[0]
    head_dim = width // heads
    nodes = node_table.shape[0]
    assert n_seq == 2 * heads and tok == BLK
    part_rows = -(-USERS * n_dp * nodes // LANES // 16) * 16
    vmem = pl.BlockSpec(memory_space=pltpu.VMEM)
    smem = pl.BlockSpec(memory_space=pltpu.SMEM)
    hbm = pl.BlockSpec(memory_space=pl.ANY)
    dma = pltpu.SemaphoreType.DMA
    bf16 = jnp.bfloat16
    layer_out, scores = pl.pallas_call(
        functools.partial(layer_kernel, n_dp, n_seq),
        out_shape=(
            jax.ShapeDtypeStruct(tokens.shape, bf16),
            jax.ShapeDtypeStruct(beam_nodes.shape, jnp.float32),
        ),
        in_specs=[hbm, vmem, hbm, vmem, hbm, smem, smem, smem, hbm, smem, vmem],
        out_specs=(vmem, vmem),
        scratch_shapes=[
            pltpu.VMEM(tokens.shape, bf16),
            pltpu.VMEM((4, width, width), bf16),
            pltpu.VMEM((width, width), bf16),
            pltpu.VMEM((n_dp, nodes, width), bf16),
            pltpu.VMEM((heads, 4, tok, head_dim), bf16),
            pltpu.VMEM((tok, width), bf16),
            pltpu.VMEM((heads, 3, tok, head_dim), bf16),
            pltpu.VMEM((heads, tok, head_dim), bf16),
            pltpu.VMEM((n_seq, tok, head_dim), bf16),
            pltpu.VMEM((heads, tok, head_dim), bf16),
            pltpu.VMEM((heads, tok, head_dim), bf16),
            pltpu.VMEM((n_seq // 2, 2 * tok, 2 * tok), jnp.float32),
            pltpu.VMEM((part_rows, LANES), bf16),
            pltpu.VMEM((n_seq, part_rows, LANES), bf16),
            pltpu.VMEM((n_dp * nodes, USERS * beam_nodes.shape[1]), bf16),
            dma,
            dma((4,)),
            dma,
            dma,
            dma((n_dp,)),
            dma((n_dp,)),
            dma((n_dp,)),
            dma((n_dp,)),
            dma((heads,)),
            dma((heads,)),
            dma((heads,)),
            dma((heads,)),
            dma((n_seq,)),
            dma((heads,)),
            dma((heads,)),
            dma((n_seq,)),
            dma((n_seq,)),
        ],
        compiler_params=pltpu.CompilerParams(
            collective_id=0, has_side_effects=True, vmem_limit_bytes=56 * 1024 * 1024
        ),
    )(
        tokens,
        in_gain.reshape(1, width),
        w_proj,
        out_gain.reshape(1, width),
        w_out,
        rab_slope,
        hist_blocks,
        hist_tail,
        node_table,
        subtree_map,
        beam_nodes,
    )
    return pl.pallas_call(
        hand_over,
        out_shape=(
            jax.ShapeDtypeStruct(layer_out.shape, bf16),
            jax.ShapeDtypeStruct(scores.shape, jnp.float32),
        ),
        in_specs=[vmem, vmem],
        out_specs=(hbm, hbm),
        scratch_shapes=[dma, dma],
    )(layer_out, scores)


def solution(mesh):
    placed = (
        P("dp", "seq", None),
        P(),
        P(),
        P(),
        P(),
        P(),
        P("dp", None),
        P("dp", None),
        P("dp", None),
        P(),
        P("dp", "seq"),
    )
    return jax.shard_map(
        functools.partial(body, mesh.shape["dp"], mesh.shape["seq"]),
        mesh=mesh,
        in_specs=placed,
        out_specs=(P("dp", "seq", None), P("dp", "seq")),
        check_vma=False,
    )
```

```python
import functools

import jax
import jax.numpy as jnp
from jax import lax
from jax.experimental import pallas as pl
from jax.experimental.pallas import tpu as pltpu
from jax.sharding import PartitionSpec as P

BLK = 128
SUBT = 64
USERS = 3
LANES = 128
MESH = pl.DeviceIdType.MESH
OFF = -1e30


def layer_norm(rows):
    centred = rows - jnp.mean(rows, axis=-1, keepdims=True)
    spread = jnp.mean(centred * centred, axis=-1, keepdims=True)
    return centred * lax.rsqrt(spread + 1e-05)


def silu_of_half(half):
    return half + half * jnp.tanh(half)


def far_first(count):
    order = []
    for step in range(count // 2):
        for offset in (count // 2 - step, count // 2 + step):
            if 0 < offset < count and offset not in order:
                order.append(offset)
    return order


def layer_kernel(
    n_dp,
    n_seq,
    x_hbm,
    in_gain_ref,
    w_proj_ref,
    out_gain_ref,
    w_out_ref,
    slope_ref,
    blocks_ref,
    tail_ref,
    table_ref,
    map_ref,
    beam_ref,
    layer_ref,
    scores_ref,
    x_ref,
    w_buf,
    w_out_buf,
    table_buf,
    sent,
    gate,
    kv,
    query,
    result,
    mix,
    mix_low,
    bias,
    part_sent,
    part_recv,
    onehot,
    x_sem,
    w_sem,
    w_out_sem,
    table_sem,
    table_send,
    table_recv,
    table_fwd,
    table_relay,
    kv_send,
    kv_recv,
    q_send,
    cross_send,
    q_recv,
    r_send,
    r_recv,
    r_low_recv,
    p_send,
    p_recv,
):
    tok, width = x_ref.shape[1:]
    heads, _, head_dim = mix.shape
    nodes = table_ref.shape[0]
    chunks = n_dp * nodes // LANES
    me = lax.axis_index("seq")
    dp = lax.axis_index("dp")
    side, mine = me // heads, me % heads
    base = side * heads
    window = heads + 2
    core = me % 2
    sibling = me + 1 - 2 * core

    def remote(src, dst, send_sem, recv_sem, where):
        return pltpu.make_async_remote_copy(
            src_ref=src,
            dst_ref=dst,
            send_sem=send_sem,
            recv_sem=recv_sem,
            device_id=where,
            device_id_type=MESH,
        )

    x_copy = pltpu.make_async_copy(x_hbm, x_ref, x_sem)
    x_copy.start()
    order = (1, 2, 3, 0)
    w_copies = {
        part: pltpu.make_async_copy(
            w_proj_ref.at[:, pl.ds(part * width, width)], w_buf.at[part], w_sem.at[part]
        )
        for part in order
    }
    for part in order:
        w_copies[part].start()

    barrier = pltpu.get_barrier_semaphore()
    for step in range(1, n_seq):
        pl.semaphore_signal(
            barrier, inc=1, device_id={"seq": (me + step) % n_seq}, device_id_type=MESH
        )
    for step in range(1, n_dp):
        pl.semaphore_signal(
            barrier, inc=1, device_id={"dp": (dp + step) % n_dp}, device_id_type=MESH
        )

    x_copy.wait()
    x_rows = x_ref[0].astype(jnp.float32)
    normed = (layer_norm(x_rows) * in_gain_ref[...]).astype(jnp.bfloat16)

    def project(part, store):
        w_copies[part].wait()
        for piece in range(heads // 2):
            columns = pl.ds(piece * 2 * head_dim, 2 * head_dim)
            out = jnp.dot(normed, w_buf[part, :, columns], preferred_element_type=jnp.float32)
            rows = silu_of_half(0.5 * out)
            if part == 1:
                rows = rows * (0.5 * head_dim ** (-0.5))
            store(piece, rows.astype(jnp.bfloat16))

    def store_heads(slot):
        def store(piece, rows):
            sent[slot, 2 * piece] = rows[:, :head_dim]
            sent[slot, 2 * piece + 1] = rows[:, head_dim:]

        return store

    waits = []
    for slot, landing, send_sem, recv_sem in (
        (0, query.at[me], q_send, q_recv.at[me]),
        (1, kv.at[0, mine], kv_send.at[0], kv_recv.at[0, mine]),
        (2, kv.at[1, mine], kv_send.at[1], kv_recv.at[1, mine]),
    ):
        project(slot + 1, store_heads(slot))
        if slot == 0:
            pl.semaphore_wait(barrier, n_seq - 1 + n_dp - 1)
        for step in range(heads):
            head = (mine + step) % heads
            if slot == 0:

                @pl.when(side == 1)
                def _():
                    remote(
                        sent.at[0, head],
                        query.at[me],
                        cross_send.at[step],
                        q_recv.at[me],
                        {"seq": head},
                    ).start()

            if step == 0:
                pltpu.make_async_copy(sent.at[slot, head], landing, recv_sem).start()
            else:
                copy = remote(
                    sent.at[slot, head], landing, send_sem.at[step], recv_sem, {"seq": base + head}
                )
                copy.start()
                waits.append(copy)

    part_nodes = nodes // 2
    for step in range(1, n_dp):
        own_rows = pl.ds(core * part_nodes, part_nodes)
        copy = remote(
            table_ref.at[own_rows],
            table_buf.at[dp, own_rows],
            table_send.at[step],
            table_recv.at[dp],
            {"dp": (dp + step) % n_dp},
        )
        copy.start()
        waits.append(copy)
    pltpu.make_async_copy(table_ref, table_buf.at[dp], table_sem).start()
    w_out_copy = pltpu.make_async_copy(w_out_ref, w_out_buf, w_out_sem)
    w_out_copy.start()

    row = lax.broadcasted_iota(jnp.int32, bias.shape, 0)
    column = lax.broadcasted_iota(jnp.int32, bias.shape, 1)
    gap = (n_seq - 1) * tok + row - column
    slope = slope_ref[mine]
    logs = jnp.log(1.0 + jnp.maximum(gap, 0).astype(jnp.float32))
    bias[...] = jnp.where(gap >= 0, (0.5 * slope) * logs, OFF)

    @pl.when(side == 0)
    def _():
        mix_low[...] = jnp.zeros_like(mix_low)

    starts = [0, blocks_ref[0, 0], blocks_ref[0, 0] + blocks_ref[0, 1]]
    lengths = [(blocks_ref[0, u] - 1) * BLK + tail_ref[0, u] for u in range(USERS)]

    def landed(ref, sem):
        pltpu.make_async_copy(ref, ref, sem).wait()

    def attend(block, first_key, low, high, bias_at):
        first = jnp.where(block >= starts[1], starts[1], 0)
        length = jnp.where(block >= starts[1], lengths[1], lengths[0])
        first = jnp.where(block >= starts[2], starts[2], first)
        length = jnp.where(block >= starts[2], lengths[2], length)
        queries = query[block]
        total = jnp.zeros((tok, head_dim), jnp.float32)
        for at in range(low, high, 2):
            end = min(at + 2, high)
            wide = (end - at) * tok
            keys = kv[0, at:end].reshape(wide, head_dim)
            values = kv[1, at:end].reshape(wide, head_dim)
            key_block = lax.broadcasted_iota(jnp.int32, (1, wide), 1) // tok + (first_key + at)
            seen = jnp.where(key_block >= first, 0.0, OFF)
            scores = lax.dot_general(
                queries, keys, (((1,), (1,)), ((), ())), preferred_element_type=jnp.float32
            )
            begin = bias_at + (at - low) * tok
            halves = scores + (bias[:, begin : begin + wide] + seen)
            weights = silu_of_half(halves).astype(jnp.bfloat16)
            total += jnp.dot(weights, values, preferred_element_type=jnp.float32)
        row = lax.broadcasted_iota(jnp.int32, (tok, head_dim), 0)
        live = (block - first) * tok + row < length
        return jnp.where(live, total, 0.0).astype(jnp.bfloat16)

    for place in range(heads):
        block = base + place
        landed(query.at[block], q_recv.at[block])
        for which in range(2):
            landed(kv.at[which, place], kv_recv.at[which, place])
        count = place + 1
        result[place] = attend(block, base, 0, count, (n_seq - count) * tok)

        @pl.when(mine != place)
        def _():
            remote(
                result.at[place], mix.at[mine], r_send.at[place], r_recv.at[mine], {"seq": block}
            ).start()

        @pl.when(mine == place)
        def _():
            pltpu.make_async_copy(result.at[place], mix.at[mine], r_recv.at[mine]).start()

    for step in range(1, n_dp):
        source = (dp + step) % n_dp
        came = table_buf.at[source, pl.ds(core * part_nodes, part_nodes)]
        landed(came, table_recv.at[source])
        copy = remote(came, came, table_fwd.at[step], table_relay.at[source], {"seq": sibling})
        copy.start()
        waits.append(copy)

    @pl.when(side == 0)
    def _():
        copies = []
        for step in range(heads):
            block = heads + step
            landed(query.at[block], q_recv.at[block])
            low = max(0, block + 1 - window)
            result[block] = attend(block, 0, low, heads, (n_seq - 1 - block + low) * tok)
            copy = remote(
                result.at[heads + step],
                mix_low.at[mine],
                r_send.at[heads + step],
                r_low_recv.at[mine],
                {"seq": block},
            )
            copy.start()
            copies.append(copy)
        for copy in copies:
            copy.wait_send()

    def store_gate(piece, rows):
        gate[:, pl.ds(piece * 2 * head_dim, 2 * head_dim)] = rows

    project(0, store_gate)

    w_out_copy.wait()
    for source in range(heads):
        landed(mix.at[source], r_recv.at[source])

    @pl.when(side == 1)
    def _():
        for source in range(heads):
            landed(mix_low.at[source], r_low_recv.at[source])

    mixed = jnp.concatenate(
        [
            mix[head].astype(jnp.float32) + mix_low[head].astype(jnp.float32)
            for head in range(heads)
        ],
        axis=1,
    )
    gated = layer_norm(mixed) * out_gain_ref[...] * gate[...].astype(jnp.float32)
    out = jnp.dot(
        gated.astype(jnp.bfloat16), w_out_buf[...], preferred_element_type=jnp.float32
    )
    layer_rows = (x_ref[0].astype(jnp.float32) + out).astype(jnp.bfloat16)

    rows = 16
    which_user = lax.broadcasted_iota(jnp.int32, (rows, tok), 0)
    slot = lax.broadcasted_iota(jnp.int32, (rows, tok), 1) + me * tok
    last = jnp.full((rows, tok), -1, jnp.int32)
    for u in range(USERS):
        last = jnp.where(which_user == u, starts[u] * BLK + lengths[u] - 1, last)
    picker = jnp.where(slot == last, 1.0, 0.0).astype(jnp.bfloat16)
    states = jnp.dot(picker, layer_rows, preferred_element_type=jnp.float32).astype(jnp.bfloat16)
    pltpu.make_async_copy(table_ref, table_buf.at[dp], table_sem).wait()
    for step in range(1, n_dp):
        source = (dp + step) % n_dp
        came = table_buf.at[source, pl.ds((1 - core) * part_nodes, part_nodes)]
        pltpu.make_async_copy(came, came, table_relay.at[source]).wait()
    node_scores = lax.dot_general(
        states,
        table_buf[...].reshape(n_dp * nodes, width),
        (((1,), (1,)), ((), ())),
        preferred_element_type=jnp.float32,
    )
    pieces = [
        node_scores[u : u + 1, c * LANES : (c + 1) * LANES]
        for u in range(USERS)
        for c in range(chunks)
    ]
    spare = part_sent.shape[0] - len(pieces)
    if spare:
        pieces.append(jnp.zeros((spare, LANES), jnp.float32))
    part = jnp.concatenate(pieces, axis=0).astype(jnp.bfloat16)
    part_sent[...] = part
    part_recv[me] = part
    for step in far_first(n_seq):
        copy = remote(
            part_sent,
            part_recv.at[me],
            p_send.at[step],
            p_recv.at[me],
            {"seq": (me + step) % n_seq},
        )
        copy.start()
        waits.append(copy)

    layer_ref[0] = layer_rows

    beams = beam_ref[...]
    subtree = beams >> 6
    found = jnp.zeros_like(beams)
    for index in range(map_ref.shape[0]):
        found = jnp.where(subtree == index, map_ref[index], found)
    stored = found * SUBT + (beams & (SUBT - 1))
    per_user = beams.shape[1]
    stored_row = jnp.concatenate([stored[u : u + 1] for u in range(USERS)], axis=1)
    node = lax.broadcasted_iota(jnp.int32, onehot.shape, 0)
    onehot[...] = jnp.where(node == stored_row, 1.0, 0.0).astype(jnp.bfloat16)

    for copy in waits:
        copy.wait_send()
    @pl.when(side == 1)
    def _():
        for step in range(heads):
            head = (mine + step) % heads
            remote(
                sent.at[0, head], query.at[me], cross_send.at[step], q_recv.at[me], {"seq": head}
            ).wait_send()

    for place in range(heads):

        @pl.when(mine != place)
        def _():
            remote(
                result.at[place],
                mix.at[mine],
                r_send.at[place],
                r_recv.at[mine],
                {"seq": base + place},
            ).wait_send()

    for step in far_first(n_seq):
        source = (me + step) % n_seq
        pltpu.make_async_copy(
            part_recv.at[source], part_recv.at[source], p_recv.at[source]
        ).wait()
    total = jnp.sum(part_recv[...].astype(jnp.float32), axis=0)
    users = [
        jnp.concatenate(
            [total[u * chunks + c : u * chunks + c + 1] for c in range(chunks)], axis=1
        )
        for u in range(USERS)
    ]
    users.append(jnp.zeros((rows - USERS, n_dp * nodes), jnp.float32))
    score_rows = jnp.concatenate(users, axis=0).astype(jnp.bfloat16)
    picked = jnp.dot(score_rows, onehot[...], preferred_element_type=jnp.float32)
    for u in range(USERS):
        scores_ref[u : u + 1] = picked[u : u + 1, u * per_user : (u + 1) * per_user]


def hand_over(layer_in, scores_in, layer_out, scores_out, layer_sem, scores_sem):
    layer = pltpu.make_async_copy(layer_in, layer_out, layer_sem)
    scores = pltpu.make_async_copy(scores_in, scores_out, scores_sem)
    layer.start()
    scores.start()
    layer.wait()
    scores.wait()


def body(
    n_dp,
    n_seq,
    tokens,
    in_gain,
    w_proj,
    out_gain,
    w_out,
    rab_slope,
    hist_blocks,
    hist_tail,
    node_table,
    subtree_map,
    beam_nodes,
):
    _, tok, width = tokens.shape
    heads = rab_slope.shape[0]
    head_dim = width // heads
    nodes = node_table.shape[0]
    assert n_seq == 2 * heads and tok == BLK
    part_rows = -(-USERS * n_dp * nodes // LANES // 16) * 16
    vmem = pl.BlockSpec(memory_space=pltpu.VMEM)
    smem = pl.BlockSpec(memory_space=pltpu.SMEM)
    hbm = pl.BlockSpec(memory_space=pl.ANY)
    dma = pltpu.SemaphoreType.DMA
    bf16 = jnp.bfloat16
    layer_out, scores = pl.pallas_call(
        functools.partial(layer_kernel, n_dp, n_seq),
        out_shape=(
            jax.ShapeDtypeStruct(tokens.shape, bf16),
            jax.ShapeDtypeStruct(beam_nodes.shape, jnp.float32),
        ),
        in_specs=[hbm, vmem, hbm, vmem, hbm, smem, smem, smem, hbm, smem, vmem],
        out_specs=(vmem, vmem),
        scratch_shapes=[
            pltpu.VMEM(tokens.shape, bf16),
            pltpu.VMEM((4, width, width), bf16),
            pltpu.VMEM((width, width), bf16),
            pltpu.VMEM((n_dp, nodes, width), bf16),
            pltpu.VMEM((3, heads, tok, head_dim), bf16),
            pltpu.VMEM((tok, width), bf16),
            pltpu.VMEM((2, heads, tok, head_dim), bf16),
            pltpu.VMEM((n_seq, tok, head_dim), bf16),
            pltpu.VMEM((n_seq, tok, head_dim), bf16),
            pltpu.VMEM((heads, tok, head_dim), bf16),
            pltpu.VMEM((heads, tok, head_dim), bf16),
            pltpu.VMEM((tok, n_seq * tok), jnp.float32),
            pltpu.VMEM((part_rows, LANES), bf16),
            pltpu.VMEM((n_seq, part_rows, LANES), bf16),
            pltpu.VMEM((n_dp * nodes, USERS * beam_nodes.shape[1]), bf16),
            dma,
            dma((4,)),
            dma,
            dma,
            dma((n_dp,)),
            dma((n_dp,)),
            dma((n_dp,)),
            dma((n_dp,)),
            dma((2, heads)),
            dma((2, heads)),
            dma((heads,)),
            dma((heads,)),
            dma((n_seq,)),
            dma((n_seq,)),
            dma((heads,)),
            dma((heads,)),
            dma((n_seq,)),
            dma((n_seq,)),
        ],
        compiler_params=pltpu.CompilerParams(
            collective_id=0, has_side_effects=True, vmem_limit_bytes=56 * 1024 * 1024
        ),
    )(
        tokens,
        in_gain.reshape(1, width),
        w_proj,
        out_gain.reshape(1, width),
        w_out,
        rab_slope,
        hist_blocks,
        hist_tail,
        node_table,
        subtree_map,
        beam_nodes,
    )
    return pl.pallas_call(
        hand_over,
        out_shape=(
            jax.ShapeDtypeStruct(layer_out.shape, bf16),
            jax.ShapeDtypeStruct(scores.shape, jnp.float32),
        ),
        in_specs=[vmem, vmem],
        out_specs=(hbm, hbm),
        scratch_shapes=[dma, dma],
    )(layer_out, scores)


def solution(mesh):
    placed = (
        P("dp", "seq", None),
        P(),
        P(),
        P(),
        P(),
        P(),
        P("dp", None),
        P("dp", None),
        P("dp", None),
        P(),
        P("dp", "seq"),
    )
    return jax.shard_map(
        functools.partial(body, mesh.shape["dp"], mesh.shape["seq"]),
        mesh=mesh,
        in_specs=placed,
        out_specs=(P("dp", "seq", None), P("dp", "seq")),
        check_vma=False,
    )
```
